128 devices in a mesh: freq: 4 (over x), tile: 32 (over z, y, core).
Axes of the slice: x: 4, y: 4, z: 4, core: 2. Of those that a mesh axis runs over, the one named last changes fastest.
Arguments:
- x_time: float32 [8192, 64, 256], P(('tile', 'freq')), may hold values from -4 to 4
- mute: int32 [8192], P(('tile', 'freq')), may hold values from 0 to 175, as said below
- ranks: int32 [4, 32, 32], P('freq'), may hold values from 8 to 64, as said below
- right_factor_columns: float32 [4, 2, 32, 256, 2048], P('freq', None, 'tile'), may hold values from -0.375 to 0.375
- u_rows: float32 [4, 2, 32, 256, 2048], P('freq', None, 'tile'), may hold values from -0.1875 to 0.1875
- data: float32 [4, 2, 8192, 64], P('freq', None, 'tile'), may hold values from -6 to 6
Outputs:
- x_out: float32 [8192, 64, 256], P(('tile', 'freq'))
- resid: float32 [4, 2, 8192, 64], P('freq', None, 'tile')
The draws below stay inside these ranges and needn't reach their ends.
Inputs may be any that keep to these rules, and one draw needn't show every extreme that they name: mute never falls with the receiver index. `ranks`: at each frequency, the 1 tile rows of some index of tile have rank 64 in every tile column.
All inputs are finite; a program needn't handle non-finite values.
Results may differ from the reference program's by a relative error of at most 0.0003.
Values sent between devices are 32-bit elements; how exact they have to be, the bound alone decides.
A program may use at most 192 MiB of HBM per device.

```python
import jax
import jax.numpy as jnp
from jax import lax

NB = 256
NV = 64
NT = 256
FLO = 16
KMAX = 64
KLO = 8
ITERS = 2
RT_DEV = 1
NF = 4
TC = 32
TR = 32
NR = 8192
NS = 8192
RCOL = 2048
RROW = 2048


def draw_mute(key, part):
    ramp = NT * 5 // 8
    jitter = jax.random.randint(key, (NR,), 0, NT // 16)
    place = jnp.arange(NR, dtype=jnp.int32)
    base = (place * ramp // NR + jitter).astype(jnp.int32)
    base = lax.cummax(base, axis=0)
    base = jnp.where(place == 0, 0, base)
    base = jnp.where(place == NR - 1, ramp + NT // 16 - 1, base)
    return base.astype(jnp.int32)


def draw_ranks(key, part):
    first, second = jax.random.split(jax.random.fold_in(key, 11))
    rows = jnp.arange(TR, dtype=jnp.int32)[:, None]
    cols = jnp.arange(TC, dtype=jnp.int32)[None, :]
    distance = jnp.abs(rows * TC - cols * TR)
    top = KMAX - (KMAX - KLO) * distance // (TR * TC)
    raw = jax.random.randint(first, (NF, TR, TC), 0, 1 << 20)
    rank = KLO + raw % (top - KLO + 1)[None]
    owner = jax.random.randint(second, (NF, 1, 1), 0, TC)
    full = rows[None] // RT_DEV == owner
    return jnp.where(full, KMAX, rank).astype(jnp.int32)


def block_levels(rng, dims, shards, smallest, largest):
    level, own = 1.0, jax.random.fold_in(rng, 6)
    for axis_at, blocks in shards:
        heights = jnp.exp(jax.random.uniform(jax.random.fold_in(own, axis_at), (blocks,), jnp.float32, smallest / len(shards), largest / len(shards)))
        level = level * jnp.repeat(heights, dims[axis_at] // blocks).reshape([-1 if axis == axis_at else 1 for axis in range(len(dims))])
    return level


def centred(rng, shape, deviation, reach, cuts=(), kind=jnp.bfloat16):
    factor_of = block_levels(rng, shape, cuts, -0.22, 0.18) if cuts else 1.0
    drawn = jax.random.normal(rng, shape, jnp.float32) * deviation * factor_of
    return jnp.minimum(jnp.maximum(drawn, -reach), reach).astype(kind)


def setup_inputs(seed: int = 0) -> dict:
    streams_of = jax.random.split(jax.random.key(seed), 7)
    return {
        "x_time": centred(streams_of[0], (NR, NV, NT), 0.5, 4.0, ((0, 128),), jnp.float32),
        "mute": draw_mute(jax.random.fold_in(streams_of[6], 71), 0),
        "ranks": draw_ranks(jax.random.fold_in(streams_of[6], 71), 0),
        "right_factor_columns": centred(streams_of[3], (NF, 2, TC, NB, RCOL), NB ** -0.5, 0.375, ((0, 4), (2, 32)), jnp.float32),
        "u_rows": centred(streams_of[4], (NF, 2, TR, NB, RROW), (TC * KMAX // 2) ** -0.5, 0.1875, ((0, 4), (2, 32)), jnp.float32),
        "data": centred(streams_of[5], (NF, 2, NS, NV), 1.0, 6.0, ((0, 4), (2, 32)), jnp.float32),
    }


HIGH = lax.Precision.HIGHEST


def mat_mul(left, right):
    return jnp.dot(left, right, precision=HIGH, preferred_element_type=jnp.float32)


def mat_tmul(left, right):
    return lax.dot_general(left, right, (((0,), (0,)), ((), ())), precision=HIGH, preferred_element_type=jnp.float32)


def conjugate_product(matrix, model_wavefield):
    real = mat_tmul(matrix[0], model_wavefield[0]) + mat_tmul(matrix[1], model_wavefield[1])
    imag = mat_tmul(matrix[0], model_wavefield[1]) - mat_tmul(matrix[1], model_wavefield[0])
    return jnp.stack([real, imag])


def direct_product(matrix, model_wavefield):
    real = mat_mul(matrix[0], model_wavefield[0]) - mat_mul(matrix[1], model_wavefield[1])
    imag = mat_mul(matrix[0], model_wavefield[1]) + mat_mul(matrix[1], model_wavefield[0])
    return jnp.stack([real, imag])


def tables():
    steps = jnp.arange(NT, dtype=jnp.int32)
    freqs = FLO + jnp.arange(NF, dtype=jnp.int32)
    phase = (freqs[:, None] * steps[None, :]) % NT
    angle = phase.astype(jnp.float32) * (2.0 * jnp.pi / NT)
    return jnp.cos(angle), jnp.sin(angle)


def forward_one(model_wavefield, v_f, u_f, rank_f):
    col_off = jnp.cumsum(rank_f, axis=0) - rank_f
    row_off = jnp.cumsum(rank_f, axis=1) - rank_f
    blocks = model_wavefield.reshape(2, TC, NB, NV)
    column_contributions = lax.map(lambda j: conjugate_product(v_f[:, j], blocks[:, j]), jnp.arange(TC, dtype=jnp.int32))
    flat = column_contributions.transpose(1, 0, 2, 3).reshape(2, TC * RCOL, NV)
    slots = jnp.arange(RROW, dtype=jnp.int32)

    def one_row(i):
        offsets = row_off[i]
        which = jnp.sum((offsets[None, :] <= slots[:, None]).astype(jnp.int32), axis=1) - 1
        inner = slots - offsets[which]
        valid = inner < rank_f[i][which]
        source = which * RCOL + col_off[i][which] + jnp.minimum(inner, KMAX - 1)
        collected_pieces = jnp.where(valid[None, :, None], flat[:, source], 0.0)
        return direct_product(u_f[:, i], collected_pieces)

    rows_out = lax.map(one_row, jnp.arange(TR, dtype=jnp.int32))
    return rows_out.transpose(1, 0, 2, 3).reshape(2, NS, NV)


def adjoint_one(resid_f, v_f, u_f, rank_f):
    col_off = jnp.cumsum(rank_f, axis=0) - rank_f
    row_off = jnp.cumsum(rank_f, axis=1) - rank_f
    blocks = resid_f.reshape(2, TR, NB, NV)
    row_terms = lax.map(lambda i: conjugate_product(u_f[:, i], blocks[:, i]), jnp.arange(TR, dtype=jnp.int32))
    flat = row_terms.transpose(1, 0, 2, 3).reshape(2, TR * RROW, NV)
    slots = jnp.arange(RCOL, dtype=jnp.int32)

    def one_column(j):
        offsets = col_off[:, j]
        which = jnp.sum((offsets[None, :] <= slots[:, None]).astype(jnp.int32), axis=1) - 1
        inner = slots - offsets[which]
        valid = inner < rank_f[:, j][which]
        source = which * RROW + row_off[:, j][which] + jnp.minimum(inner, KMAX - 1)
        collected_pieces = jnp.where(valid[None, :, None], flat[:, source], 0.0)
        return direct_product(v_f[:, j], collected_pieces)

    cols_out = lax.map(one_column, jnp.arange(TC, dtype=jnp.int32))
    return cols_out.transpose(1, 0, 2, 3).reshape(2, NR, NV)


def reference(x_time, mute, ranks, right_factor_columns, u_rows, data):
    cosines, sines = tables()
    keep = (jnp.arange(NT, dtype=jnp.int32)[None, :] >= mute[:, None]).astype(jnp.float32)

    def spectra(model_wavefield):
        real = jnp.einsum('rvt,ft->frv', model_wavefield, cosines, precision=HIGH, preferred_element_type=jnp.float32)
        imag = -jnp.einsum('rvt,ft->frv', model_wavefield, sines, precision=HIGH, preferred_element_type=jnp.float32)
        return jnp.stack([real, imag], axis=1)

    def apply_all(model_wavefield):
        spec = spectra(model_wavefield)
        return jnp.stack([forward_one(spec[f], right_factor_columns[f], u_rows[f], ranks[f]) for f in range(NF)])

    def adjoint_all(resid):
        spec = jnp.stack([adjoint_one(resid[f], right_factor_columns[f], u_rows[f], ranks[f]) for f in range(NF)])
        real = jnp.einsum('frv,ft->rvt', spec[:, 0], cosines, precision=HIGH, preferred_element_type=jnp.float32)
        imag = jnp.einsum('frv,ft->rvt', spec[:, 1], sines, precision=HIGH, preferred_element_type=jnp.float32)
        return (real - imag) * keep[:, None, :]

    x_out = x_time
    resid = apply_all(x_time) - data
    for step in range(ITERS):
        grad = adjoint_all(resid)
        image = apply_all(grad)
        alpha = jnp.sum(grad * grad) / jnp.sum(image * image)
        x_out = x_out - alpha * grad
        resid = resid - alpha * image
    return x_out, resid
```

```python
import functools

import jax
import jax.numpy as jnp
import numpy as np
from jax import lax
from jax.experimental import pallas as pl
from jax.experimental.pallas import tpu as pltpu
from jax.sharding import PartitionSpec as P

FLO = 16
MESH = pl.DeviceIdType.MESH
F32, BF16 = jnp.float32, jnp.bfloat16
NF, NTILE, KMAX, NB, NV, NT, BLK = 4, 32, 64, 256, 64, 256, 64
NG = 8


def basis():
    steps = np.arange(NT)
    freqs = FLO + np.arange(NF)
    angle = (freqs[:, None] * steps[None, :] % NT).astype(np.float32) * np.float32(2.0 * np.pi / NT)
    return np.concatenate([np.cos(angle), -np.sin(angle)]).astype(np.float32)


def split(a):
    hi = a.astype(BF16)
    return hi, (a - hi.astype(F32)).astype(BF16)


def dot(a, b, dims=((1,), (0,))):
    return lax.dot_general(a, b, (dims, ((), ())), preferred_element_type=F32)


def swap(a):
    lane = lax.broadcasted_iota(jnp.int32, a.shape, 1)
    r = pltpu.roll(a, 64, 1)
    return jnp.where(lane < 64, r, -r)


def rhs(a, sign):
    b = sign * swap(a)
    ah, al = split(a)
    bh, bl = split(b)
    return jnp.concatenate([jnp.concatenate([ah, al], 1), jnp.concatenate([bh, bl], 1)], 0)


def three(o):
    return o[:256, :128] + o[:256, 128:] + o[256:, :128]


def setup_kernel(me_ref, ranks_ref, x_hbm, v_hbm, u_hbm, bb_ref, spec_ref, vt_hbm, ut_hbm, x_buf, raw, tall, packed, ld_sem, st_sem):
    me = me_ref[0]
    loads = []
    for m, hbm in enumerate((v_hbm, u_hbm)):
        for c in range(2):
            loads.append(pltpu.make_async_copy(hbm.at[c], raw.at[m, c], ld_sem.at[m * 2 + c]))
    loads.append(pltpu.make_async_copy(x_hbm, x_buf, ld_sem.at[4]))
    for cp in loads:
        cp.start()

    def flip(m):
        for c in range(2):
            loads[m * 2 + c].wait()

            @pl.loop(0, 16)
            def _(b):
                cols = pl.ds(pl.multiple_of(b * 128, 128), 128)
                turned = raw[m, c, :, cols].T
                tall[c, 0, cols, :] = turned[:, :128]
                tall[c, 1, cols, :] = turned[:, 128:]

    def store(m, g):
        return pltpu.make_async_copy(packed.at[m, g], (vt_hbm, ut_hbm)[m].at[g], st_sem.at[m, g])

    def pack(m, rank_at):
        def one(g, off):
            for j in range(4):
                k = rank_at(g * 4 + j)
                for c in range(2):
                    piece = jnp.concatenate([tall[c, h, pl.ds(off, 64), :] for h in range(2)], 1)
                    slot = lax.broadcasted_iota(jnp.int32, (64, NB), 0)
                    hi, lo = split(jnp.where(slot < k, piece, 0.0))
                    packed[m, g, j * 64:(j + 1) * 64, c * 256:(c + 1) * 256] = hi
                    packed[m, g, 256 + j * 64:256 + (j + 1) * 64, c * 256:(c + 1) * 256] = lo
                off = off + k
            store(m, g).start()
            return off

        lax.fori_loop(0, NG, one, jnp.int32(0))

    flip(0)
    pack(0, lambda i: ranks_ref[i, me])
    flip(1)
    pack(1, lambda j: ranks_ref[me, j])
    loads[4].wait()
    bb = bb_ref[...]

    @pl.loop(0, 16)
    def _(k):
        hi, lo = split(x_buf[pl.ds(pl.multiple_of(k * 256, 256), 256), :])
        o1 = dot(bb, hi, ((1,), (1,)))
        o2 = dot(bb, lo, ((1,), (1,)))
        o = o1[:8] + o1[8:] + o2[:8]
        for r in range(4):
            row = jnp.concatenate([o[:4, r * 64:(r + 1) * 64], o[4:, r * 64:(r + 1) * 64]], 1)
            spec_ref[pl.ds(k * 4 + r, 4, stride=64), :] = row

    for m in range(2):
        @pl.loop(0, NG)
        def _(g):
            store(m, g).wait()


def main_kernel(
    mute_ref, spec_ref, vt_hbm, ut_hbm, data_ref, prod_ref,
    comb_ref, resid_ref,
    vt, vn, ut, un, wbuf, zbuf, fsend, frecv, spec0, right, acc,
    gmap, r0_ref, im_ref, sc_send, sc_recv, sc2_send, sc2_recv,
    ld_sem, ts_sem, tr_sem, fs_sem, fr_sem, ss_sem, sr_sem, s2s_sem, s2r_sem,
):
    me = lax.axis_index("tile")
    fme = lax.axis_index("freq")
    mygroup = me // 4

    loads = [pltpu.make_async_copy(vt_hbm, vt, ld_sem.at[0]), pltpu.make_async_copy(ut_hbm, ut, ld_sem.at[1])]
    for cp in loads:
        cp.start()

    def setup_wide(t_ref, n_ref):
        @pl.loop(0, NG)
        def _(g):
            for p in range(2):
                for c in range(2):
                    n_ref[g, p * 256:(p + 1) * 256, c * 256:(c + 1) * 256] = (
                        t_ref[g, p * 256:(p + 1) * 256, c * 256:(c + 1) * 256].T)

    bar = pltpu.get_barrier_semaphore()

    @pl.loop(1, NTILE)
    def _(d):
        pl.semaphore_signal(bar, inc=1, device_id={"tile": lax.rem(me + d, NTILE)}, device_id_type=MESH)

    for d in range(1, NF):
        pl.semaphore_signal(bar, inc=1, device_id={"freq": lax.rem(fme + d, NF)}, device_id_type=MESH)

    fsend[0] = spec_ref[...]
    pl.semaphore_wait(bar, NTILE - 1 + NF - 1)

    def fcopy(e, peer, at):
        return pltpu.make_async_remote_copy(
            src_ref=fsend.at[e, pl.ds(pl.multiple_of(peer * 64, 64), 64)],
            dst_ref=frecv.at[e, pl.ds(pl.multiple_of(at * 64, 64), 64)],
            send_sem=fs_sem.at[e, peer], recv_sem=fr_sem.at[e, at],
            device_id={"freq": peer}, device_id_type=MESH)

    def fstart(e):
        for d in range(1, NF):
            fcopy(e, lax.rem(fme + d, NF), fme).start()

    def fwait(e):
        for d in range(1, NF):
            peer = lax.rem(fme + d, NF)
            fcopy(e, peer, peer).wait()
        own = pl.ds(pl.multiple_of(fme * 64, 64), 64)
        frecv[e, own, :] = fsend[e, own, :]

    fstart(0)

    def tcopy(e, peer, at):
        return pltpu.make_async_remote_copy(
            src_ref=wbuf.at[e, peer], dst_ref=zbuf.at[e, at],
            send_sem=ts_sem.at[e, peer], recv_sem=tr_sem.at[e, at],
            device_id={"tile": peer}, device_id_type=MESH)

    inner = lax.rem(me, 4)

    def mate(d):
        return mygroup * 4 + lax.rem(inner + d, 4)

    def send_products(e, t_ref):
        def products(g):
            w = three(dot(t_ref[g], right[...]))
            for j in range(4):
                wbuf[e, g * 4 + j] = w[j * 64:(j + 1) * 64]

        products(mygroup)
        for d in range(1, 4):
            tcopy(e, mate(d), me).start()

        @pl.loop(1, NG)
        def _(k):
            g = lax.rem(mygroup + k, NG)
            products(g)
            for j in range(4):
                tcopy(e, g * 4 + j, me).start()

    def gather_products(e, n_ref):
        for d in range(1, 4):
            tcopy(e, mate(d), mate(d)).wait_recv()
        zbuf[e, me] = wbuf[e, me]
        z = zbuf[e, pl.ds(mygroup * 4, 4)].reshape(256, 128)
        acc[...] = dot(n_ref[mygroup], rhs(z, -1.0))

        @pl.loop(1, NG)
        def _(k):
            g = lax.rem(mygroup + NG - k, NG)
            for j in range(4):
                tcopy(e, g * 4 + j, g * 4 + j).wait_recv()
            z = zbuf[e, pl.ds(g * 4, 4)].reshape(256, 128)
            acc[...] += dot(n_ref[g], rhs(z, -1.0))

        return three(acc[...])

    def sent(e):
        @pl.loop(1, NTILE)
        def _(d):
            peer = lax.rem(me + d, NTILE)
            tcopy(e, peer, peer).wait_send()

    def scopy(n, peer, at):
        return pltpu.make_async_remote_copy(
            src_ref=sc_send.at[n], dst_ref=sc_recv.at[n, at],
            send_sem=ss_sem.at[n, peer], recv_sem=sr_sem.at[n, at],
            device_id={"tile": peer}, device_id_type=MESH)

    def s2copy(n, peer, at):
        return pltpu.make_async_remote_copy(
            src_ref=sc2_send.at[n], dst_ref=sc2_recv.at[n, at],
            send_sem=s2s_sem.at[n, peer], recv_sem=s2r_sem.at[n, at],
            device_id={"freq": peer}, device_id_type=MESH)

    def sum_start(n, gn, im):
        row = lax.broadcasted_iota(jnp.int32, (8, 128), 0)
        inn = jnp.sum(im * im, axis=0, keepdims=True)
        mine = jnp.where(row == 0, gn, jnp.where(row == 1, inn, 0.0))
        sc_send[n] = mine

        @pl.loop(1, NTILE)
        def _(d):
            scopy(n, lax.rem(me + d, NTILE), me).start()

    def sum_middle(n):
        @pl.loop(1, NTILE)
        def _(d):
            peer = lax.rem(me + d, NTILE)
            scopy(n, peer, peer).wait()

        sc_recv[n, me] = sc_send[n]
        part = jnp.sum(sc_recv[n], axis=0)
        sc2_send[n] = part
        for d in range(1, NF):
            s2copy(n, lax.rem(fme + d, NF), fme).start()

    def sum_end(n):
        for d in range(1, NF):
            peer = lax.rem(fme + d, NF)
            s2copy(n, peer, peer).wait()
        sc2_recv[n, fme] = sc2_send[n]
        both = jnp.sum(jnp.sum(sc2_recv[n], axis=0), axis=1, keepdims=True)
        return both[0:1] / both[1:2]

    def setup_gram():
        t = lax.broadcasted_iota(jnp.int32, (BLK, NT), 1)
        keep = (t >= mute_ref[...]).astype(F32)
        gram = jnp.dot(keep, prod_ref[...], precision=lax.Precision.HIGHEST, preferred_element_type=F32)
        lane = lax.broadcasted_iota(jnp.int32, (BLK, 128), 1)
        for fo in range(NF):
            for fi in range(NF):
                def col(a, b):
                    return jnp.broadcast_to(gram[:, a * 8 + b:a * 8 + b + 1], (BLK, 128))
                gmap[fo, fi, 0] = jnp.where(lane < 64, col(fo, fi), col(4 + fo, 4 + fi))
                gmap[fo, fi, 1] = jnp.where(lane < 64, col(fo, 4 + fi), col(4 + fo, fi))

    def mix(e_out, spec):
        rolled = [pltpu.roll(s, 64, 1) for s in spec]
        total = jnp.zeros((1, 128), F32)
        for fo in range(NF):
            o = jnp.zeros((BLK, 128), F32)
            for fi in range(NF):
                o += gmap[fo, fi, 0] * spec[fi] + gmap[fo, fi, 1] * rolled[fi]
            fsend[e_out, pl.ds(fo * 64, 64), :] = o
            total += jnp.sum(spec[fo] * o, axis=0, keepdims=True)
        return total

    def read_spec(e):
        return [frecv[e, pl.ds(f * 64, 64), :] for f in range(NF)]

    loads[0].wait()
    fwait(0)
    right[...] = rhs(frecv[0], 1.0)
    send_products(0, vt)
    loads[1].wait()
    setup_wide(ut, un)
    r0 = gather_products(0, un) - jnp.concatenate([data_ref[0], data_ref[1]], 1)
    r0_ref[...] = r0

    right[...] = rhs(r0, 1.0)
    send_products(1, ut)
    setup_wide(vt, vn)
    setup_gram()
    fsend[1] = gather_products(1, vn)
    fstart(1)
    fwait(1)
    s0 = read_spec(1)
    gn0 = mix(2, s0)
    fstart(2)
    for f in range(NF):
        spec0[f] = s0[f]
    fwait(2)
    right[...] = rhs(frecv[2], 1.0)
    send_products(2, vt)
    im0 = gather_products(2, un)
    im_ref[...] = im0
    sum_start(0, gn0, im0)

    right[...] = rhs(im0, 1.0)
    send_products(3, ut)
    sum_middle(0)
    fsend[3] = gather_products(3, vn)
    fstart(3)
    alpha0 = sum_end(0)
    fwait(3)
    q = read_spec(3)
    s1 = [spec0[f] - alpha0 * q[f] for f in range(NF)]
    gn1 = mix(4, s1)
    fstart(4)
    for f in range(NF):
        comb_ref[pl.ds(f * 64, 64), :] = s1[f]
    fwait(4)
    right[...] = rhs(frecv[4], 1.0)
    send_products(4, vt)
    im1 = gather_products(4, un)
    sum_start(1, gn1, im1)
    for e in range(5):
        sent(e)
    part = r0_ref[...] - alpha0 * im_ref[...]
    sum_middle(1)
    alpha1 = sum_end(1)
    out = part - alpha1 * im1
    resid_ref[0] = out[:, :64]
    resid_ref[1] = out[:, 64:]
    for f in range(NF):
        rows = pl.ds(f * 64, 64)
        comb_ref[rows, :] = alpha0 * spec0[f] + alpha1 * comb_ref[rows, :]


def final_kernel(mute_ref, comb_ref, b3_ref, x_ref, o_ref):
    g = pl.program_id(0)
    nr = x_ref.shape[0]
    b3 = b3_ref[...]
    t = lax.broadcasted_iota(jnp.int32, (NV, NT), 1)
    for p in range(0, nr, 2):
        cols = []
        for r in (p, p + 1):
            row = comb_ref[pl.ds(g * nr + r, 4, stride=64), :]
            cols.append(jnp.concatenate([row[:, :64], row[:, 64:]], 0))
        c = jnp.concatenate(cols, 1)
        hi, lo = split(c)
        hi, lo = hi.astype(F32), lo.astype(F32)
        lhs = jnp.concatenate([hi, lo, hi, jnp.zeros_like(hi)], 0)
        grad = dot(lhs.T.astype(BF16), b3)
        for i, r in enumerate((p, p + 1)):
            o_ref[r] = x_ref[r] - jnp.where(t >= mute_ref[g * nr + r], grad[i * 64:(i + 1) * 64], 0.0)


def body(x_time, mute, ranks, right_factor_columns, u_rows, data):
    b = basis()
    bj = jnp.asarray(b)
    bhi, blo = split(bj)
    bb = jnp.concatenate([bhi, blo], 0)
    b3 = jnp.concatenate([bhi, bhi, blo, jnp.zeros_like(bhi)], 0)
    prod = jnp.asarray((b[:, None, :] * b[None, :, :]).reshape(64, NT).T)
    prod = jnp.pad(prod, ((0, 0), (0, 64)))
    vmem = pl.BlockSpec(memory_space=pltpu.VMEM)
    hbm = pl.BlockSpec(memory_space=pl.ANY)
    smem = pl.BlockSpec(memory_space=pltpu.SMEM)
    dma = pltpu.SemaphoreType.DMA
    packed = jax.ShapeDtypeStruct((NG, 512, 512), BF16)
    spec, vt, ut = pl.pallas_call(
        setup_kernel,
        out_shape=(jax.ShapeDtypeStruct((256, 128), F32), packed, packed),
        in_specs=[smem, smem, hbm, hbm, hbm, vmem],
        out_specs=(vmem, hbm, hbm),
        scratch_shapes=[
            pltpu.VMEM((4096, 256), F32),
            pltpu.VMEM((2, 2, 256, 2048), F32),
            pltpu.VMEM((2, 2, 2048, 128), F32),
            pltpu.VMEM((2, NG, 512, 512), BF16),
            dma((5,)), dma((2, NG)),
        ],
        compiler_params=pltpu.CompilerParams(vmem_limit_bytes=40 << 20),
        name="setup",
    )(lax.axis_index("tile").reshape(1), ranks[0], x_time.reshape(4096, 256), right_factor_columns[0, :, 0], u_rows[0, :, 0], bb)
    comb, resid = pl.pallas_call(
        main_kernel,
        out_shape=(jax.ShapeDtypeStruct((256, 128), F32), jax.ShapeDtypeStruct((2, 256, 64), F32)),
        in_specs=[vmem, vmem, hbm, hbm, vmem, vmem],
        out_specs=(vmem, vmem),
        scratch_shapes=[
            pltpu.VMEM((NG, 512, 512), BF16),
            pltpu.VMEM((NG, 512, 512), BF16),
            pltpu.VMEM((NG, 512, 512), BF16),
            pltpu.VMEM((NG, 512, 512), BF16),
            pltpu.VMEM((5, NTILE, 64, 128), F32),
            pltpu.VMEM((5, NTILE, 64, 128), F32),
            pltpu.VMEM((5, 256, 128), F32),
            pltpu.VMEM((5, 256, 128), F32),
            pltpu.VMEM((NF, 64, 128), F32),
            pltpu.VMEM((512, 256), BF16),
            pltpu.VMEM((512, 256), F32),
            pltpu.VMEM((NF, NF, 2, BLK, 128), F32),
            pltpu.VMEM((256, 128), F32),
            pltpu.VMEM((256, 128), F32),
            pltpu.VMEM((2, 8, 128), F32),
            pltpu.VMEM((2, NTILE, 8, 128), F32),
            pltpu.VMEM((2, 8, 128), F32),
            pltpu.VMEM((2, NF, 8, 128), F32),
            dma((2,)), dma((5, NTILE)), dma((5, NTILE)), dma((5, NF)), dma((5, NF)),
            dma((2, NTILE)), dma((2, NTILE)), dma((2, NF)), dma((2, NF)),
        ],
        compiler_params=pltpu.CompilerParams(collective_id=0, has_side_effects=True, vmem_limit_bytes=56 << 20),
        name="descent",
    )(mute[:, None], spec, vt, ut, data[0], prod)
    step = 16
    x_out = pl.pallas_call(
        final_kernel,
        grid=(BLK // step,),
        out_shape=jax.ShapeDtypeStruct((BLK, NV, NT), F32),
        in_specs=[
            smem, vmem, vmem,
            pl.BlockSpec((step, NV, NT), lambda i: (i, 0, 0)),
        ],
        out_specs=pl.BlockSpec((step, NV, NT), lambda i: (i, 0, 0)),
        compiler_params=pltpu.CompilerParams(vmem_limit_bytes=32 << 20),
        name="update",
    )(mute, comb, b3, x_time)
    return x_out, resid[None]


def solution(mesh):
    in_specs = (
        P(("tile", "freq"), None, None),
        P(("tile", "freq")),
        P("freq", None, None),
        P("freq", None, "tile", None, None),
        P("freq", None, "tile", None, None),
        P("freq", None, "tile", None),
    )
    out_specs = (P(("tile", "freq"), None, None), P("freq", None, "tile", None))
    return jax.shard_map(body, mesh=mesh, in_specs=in_specs, out_specs=out_specs, check_vma=False)
```

```python
import jax
import jax.numpy as jnp
import numpy as np
from jax import lax
from jax.experimental import pallas as pl
from jax.experimental.pallas import tpu as pltpu
from jax.sharding import PartitionSpec as P

FLO = 16
MESH = pl.DeviceIdType.MESH
F32, BF16 = jnp.float32, jnp.bfloat16
NF, NTILE, NB, NV, NT, BLK = 4, 32, 256, 64, 256, 64
NG = 8
ROOM = 60 << 20

FIRST = ((2, 2), (2, 1), (1, 2), (1, 1), (1, 3), (2, 0), (1, 0), (0, 1))
SECOND = ((0, 0), (2, 3), (3, 2), (3, 3), (3, 1), (0, 2), (3, 0), (0, 3))
OWN = 2


def basis():
    steps = np.arange(NT)
    freqs = FLO + np.arange(NF)
    angle = (freqs[:, None] * steps[None, :] % NT).astype(np.float32) * np.float32(2.0 * np.pi / NT)
    return np.concatenate([np.cos(angle), -np.sin(angle)]).astype(np.float32)


def split(a):
    hi = a.astype(BF16)
    return hi, (a - hi.astype(F32)).astype(BF16)


def dot(a, b, dims=((1,), (0,))):
    return lax.dot_general(a, b, (dims, ((), ())), preferred_element_type=F32)


def lanes(shape):
    return lax.broadcasted_iota(jnp.int32, shape, 1)


def even(shape):
    return lax.rem(lanes(shape), 64) < 32


def swap(p):
    return jnp.where(even(p.shape), pltpu.roll(p, 96, 1), pltpu.roll(p, 32, 1))


def rhs(p, sign):
    left = lanes(p.shape) < 64
    s = swap(p)
    out = []
    for q in (p, jnp.where(even(p.shape), sign * s, -sign * s)):
        hi = q.astype(BF16).astype(F32)
        lo = q - hi
        out.append(jnp.where(left, hi, pltpu.roll(lo, 64, 1)).astype(BF16))
        out.append(jnp.where(left, pltpu.roll(hi, 64, 1), lo).astype(BF16))
    return jnp.concatenate(out, 0)


def pack(o):
    s = o[:256] + o[256:]
    s = s + pltpu.roll(s, 64, 1)
    return jnp.where(lanes((128, 128)) < 64, s[:128], s[128:])


def setup_kernel(me_ref, perm_ref, ranks_ref, x_hbm, v_hbm, u_hbm, bb_ref, spec_ref, vt_hbm, ut_hbm, x_buf, raw, tall, packed, offs, ld_sem, st_sem):
    me = me_ref[0]
    loads = [pltpu.make_async_copy(x_hbm, x_buf, ld_sem.at[4])]
    for m, hbm in enumerate((v_hbm, u_hbm)):
        for c in range(2):
            loads.append(pltpu.make_async_copy(hbm.at[c], raw.at[m, c], ld_sem.at[m * 2 + c]))
    for cp in loads:
        cp.start()

    def offsets(m, rank_at):
        def one(i, off):
            offs[m, i] = off
            return off + rank_at(i)

        lax.fori_loop(0, NTILE, one, jnp.int32(0))

    ranks_at = (lambda i: ranks_ref[i, me]), (lambda j: ranks_ref[me, j])
    offsets(0, ranks_at[0])
    offsets(1, ranks_at[1])

    def flip(m):
        for c in range(2):
            loads[1 + m * 2 + c].wait()

            @pl.loop(0, 16)
            def _(b):
                cols = pl.ds(pl.multiple_of(b * 128, 128), 128)
                order = [64 * i for i in range(4)] + [64 * i + 32 for i in range(4)]
                turned = jnp.concatenate([raw[m, c, i:i + 32, cols] for i in order], 0).T
                tall[c, 0, cols, :] = turned[:, :128]
                tall[c, 1, cols, :] = turned[:, 128:]

    def store(m, g):
        return pltpu.make_async_copy(packed.at[m, g], (vt_hbm, ut_hbm)[m].at[g], st_sem.at[m, g])

    def pad(m):
        @pl.loop(0, NG)
        def _(g):
            for j in range(4):
                tile = perm_ref[g * 4 + j]
                k = ranks_at[m](tile)
                off = offs[m, tile]
                for c in range(2):
                    piece = jnp.concatenate([tall[c, h, pl.ds(off, 64), :] for h in range(2)], 1)
                    slot = lax.broadcasted_iota(jnp.int32, (64, NB), 0)
                    for n, part in enumerate(split(jnp.where(slot < k, piece, 0.0))):
                        for h in range(2):
                            at = n * 256 + h * 128 + j * 32
                            packed[m, g, at:at + 32, c * 256:(c + 1) * 256] = part[h * 32:(h + 1) * 32]
            store(m, g).start()

    loads[0].wait()
    bb = bb_ref[...]
    quarter = even((4, 128))

    @pl.loop(0, BLK // 4)
    def _(k):
        low = pl.multiple_of(k * 128, 128)
        a, b = x_buf[pl.ds(low, 128), :], x_buf[pl.ds(BLK * 32 + low, 128), :]
        hi, lo = split(jnp.concatenate([a[:64], b[:64], a[64:], b[64:]], 0))
        o1 = dot(bb, hi, ((1,), (1,)))
        o2 = dot(bb, lo, ((1,), (1,)))
        o = o1[:8] + o1[8:] + o2[:8]
        for i in range(2):
            re, im = o[:4, i * 128:(i + 1) * 128], o[4:, i * 128:(i + 1) * 128]
            rows = pl.ds(k * 2 + i, 4, stride=32)
            spec_ref[0, rows, :] = jnp.where(quarter, re, pltpu.roll(im, 32, 1))
            spec_ref[1, rows, :] = jnp.where(quarter, pltpu.roll(re, 96, 1), im)

    for m in range(2):
        flip(m)
        pad(m)
    for m in range(2):
        @pl.loop(0, NG)
        def _(g):
            store(m, g).wait()


def main_kernel(
    mute_ref, spec_ref, vt_hbm, ut_hbm, data_ref, prod_ref,
    comb_ref, resid_ref,
    vt, vn, ut, un, wbuf, zbuf, fsend, frecv, spec0, right, acc,
    keep_ref, gmap, r0_ref, im_ref, gn_ref, sc_send, sc_recv, sc2_send, sc2_recv,
    ld_sem, ts_sem, tr_sem, fs_sem, fr_sem, ss_sem, sr_sem, s2s_sem, s2r_sem,
):
    me = lax.axis_index("tile")
    fme = lax.axis_index("freq")
    my_z, my_y, my_c = me // 8, lax.rem(me // 2, 4), lax.rem(me, 2)

    loads = [pltpu.make_async_copy(vt_hbm, vt, ld_sem.at[0]), pltpu.make_async_copy(ut_hbm, ut, ld_sem.at[1])]
    for cp in loads:
        cp.start()

    bar = pltpu.get_barrier_semaphore()

    @pl.loop(1, NTILE)
    def _(d):
        pl.semaphore_signal(bar, inc=1, device_id={"tile": lax.rem(me + d, NTILE)}, device_id_type=MESH)

    for d in range(1, NF):
        pl.semaphore_signal(bar, inc=1, device_id={"freq": lax.rem(fme + d, NF)}, device_id_type=MESH)

    def setup_wide(t_ref, n_ref):
        @pl.loop(0, NG)
        def _(g):
            for p in range(2):
                for c in range(2):
                    n_ref[g, p * 256:(p + 1) * 256, c * 256:(c + 1) * 256] = (
                        t_ref[g, p * 256:(p + 1) * 256, c * 256:(c + 1) * 256].T)

    def fcopy(e, h, peer, at):
        return pltpu.make_async_remote_copy(
            src_ref=fsend.at[e, h, pl.ds(pl.multiple_of(peer * 32, 32), 32)],
            dst_ref=frecv.at[e, h, pl.ds(pl.multiple_of(at * 32, 32), 32)],
            send_sem=fs_sem.at[e, h, peer], recv_sem=fr_sem.at[e, h, at],
            device_id={"freq": peer}, device_id_type=MESH)

    def fstart(e, h):
        for d in (2, 1, 3):
            fcopy(e, h, lax.rem(fme + d, NF), fme).start()

    def fwait(e, h):
        for d in range(1, NF):
            peer = lax.rem(fme + d, NF)
            fcopy(e, h, peer, peer).wait()
        own = pl.ds(pl.multiple_of(fme * 32, 32), 32)
        frecv[e, h, own, :] = fsend[e, h, own, :]

    def offset(g, half):
        table = (FIRST, SECOND)[half]
        dz, dy = jnp.int32(table[0][0]), jnp.int32(table[0][1])
        for i in range(1, NG):
            dz, dy = jnp.where(g == i, table[i][0], dz), jnp.where(g == i, table[i][1], dy)
        return dz, dy

    def tcopy(e, h, g, j):
        half, dc = j // 2, j % 2
        dz, dy = offset(g, half)
        peer = lax.rem(my_z + dz, 4) * 8 + lax.rem(my_y + dy, 4) * 2 + lax.rem(my_c + dc, 2)
        same = jnp.logical_or(g == 0, g == 5)
        slot = g * 4 + jnp.where(same, half, 1 - half) * 2 + dc
        return pltpu.make_async_remote_copy(
            src_ref=wbuf.at[e, h, g * 4 + j], dst_ref=zbuf.at[e, h, slot],
            send_sem=ts_sem.at[e, h, g * 4 + j], recv_sem=tr_sem.at[e, h, slot],
            device_id={"tile": peer}, device_id_type=MESH)

    def arrival(e, h, p):
        return pltpu.make_async_remote_copy(
            src_ref=wbuf.at[e, h, p], dst_ref=zbuf.at[e, h, p],
            send_sem=ts_sem.at[e, h, p], recv_sem=tr_sem.at[e, h, p],
            device_id={"tile": lax.rem(me + 1, NTILE)}, device_id_type=MESH)

    def send_products(e, h, t_ref, p, sign=1.0):
        right[...] = rhs(p, sign)

        @pl.loop(0, NG // 2)
        def _(k):
            o = dot(t_ref[pl.ds(k * 2, 2)].reshape(1024, 512), right[...])
            for i in range(2):
                g = k * 2 + i
                wbuf[e, h, pl.ds(g * 4, 4)] = pack(o[i * 512:(i + 1) * 512]).reshape(4, 32, 128)
            for j in (0, 1, 3):
                tcopy(e, h, k * 2, j).start()

            @pl.when(k > 0)
            def _():
                tcopy(e, h, k * 2, OWN).start()

            for j in range(4):
                tcopy(e, h, k * 2 + 1, j).start()

    def gather_products(e, h, n_ref):
        @pl.loop(0, NG // 2)
        def _(k):
            for j in range(8):
                if j != OWN:
                    arrival(e, h, k * 8 + j).wait_recv()

            @pl.when(k > 0)
            def _():
                arrival(e, h, k * 8 + OWN).wait_recv()

            @pl.when(k == 0)
            def _():
                zbuf[e, h, OWN] = wbuf[e, h, OWN]
                acc[...] = jnp.zeros_like(acc)

            a = zbuf[e, h, pl.ds(k * 8, 4)].reshape(128, 128)
            b = zbuf[e, h, pl.ds(k * 8 + 4, 4)].reshape(128, 128)
            acc[...] += dot(n_ref[k * 2], rhs(a, -1.0)) + dot(n_ref[k * 2 + 1], rhs(b, -1.0))

        return pack(acc[...])

    def sent(e, h):
        @pl.loop(0, NTILE)
        def _(p):
            @pl.when(p != OWN)
            def _():
                arrival(e, h, p).wait_send()

    def scopy(n, peer, at):
        return pltpu.make_async_remote_copy(
            src_ref=sc_send.at[n], dst_ref=sc_recv.at[n, at],
            send_sem=ss_sem.at[n, peer], recv_sem=sr_sem.at[n, at],
            device_id={"tile": peer}, device_id_type=MESH)

    def s2copy(n, peer, at):
        return pltpu.make_async_remote_copy(
            src_ref=sc2_send.at[n], dst_ref=sc2_recv.at[n, at],
            send_sem=s2s_sem.at[n, peer], recv_sem=s2r_sem.at[n, at],
            device_id={"freq": peer}, device_id_type=MESH)

    def sum_start(n, gn, im):
        row = lax.broadcasted_iota(jnp.int32, (8, 128), 0)
        inn = sum(jnp.sum(i * i, axis=0, keepdims=True) for i in im)
        sc_send[n] = jnp.where(row == 0, gn, jnp.where(row == 1, inn, 0.0))

        @pl.loop(1, NTILE)
        def _(d):
            scopy(n, lax.rem(me + d, NTILE), me).start()

    def sum_middle(n):
        @pl.loop(1, NTILE)
        def _(d):
            peer = lax.rem(me + d, NTILE)
            scopy(n, peer, peer).wait()

        sc_recv[n, me] = sc_send[n]
        part = jnp.sum(sc_recv[n], axis=0)
        sc2_send[n] = part
        for d in range(1, NF):
            s2copy(n, lax.rem(fme + d, NF), fme).start()

    def sum_end(n):
        for d in range(1, NF):
            peer = lax.rem(fme + d, NF)
            s2copy(n, peer, peer).wait()
        sc2_recv[n, fme] = sc2_send[n]
        both = jnp.sum(jnp.sum(sc2_recv[n], axis=0), axis=1, keepdims=True)
        return both[0:1] / both[1:2]

    def setup_gram():
        @pl.loop(0, BLK)
        def _(r):
            t = lanes((1, NT))
            keep_ref[pl.ds(r, 1), :] = (t >= mute_ref[r]).astype(F32)

        gram = jnp.dot(keep_ref[...], prod_ref[...], precision=lax.Precision.HIGHEST, preferred_element_type=F32)
        lane = lanes((32, 128))
        left, real = lane < 64, even((32, 128))

        def col(a, b):
            i = a * 8 + b
            return jnp.where(left, gram[:32, i:i + 1], gram[32:, i:i + 1])

        for fo in range(NF):
            for fi in range(NF):
                gmap[fo, fi, 0] = jnp.where(real, col(fo, fi), col(4 + fo, 4 + fi))
                gmap[fo, fi, 1] = jnp.where(real, col(fo, 4 + fi), col(4 + fo, fi))

    def mix(e, h, spec):
        swapped = [swap(s) for s in spec]
        total = jnp.zeros((1, 128), F32)
        for fo in range(NF):
            o = jnp.zeros((32, 128), F32)
            for fi in range(NF):
                o += gmap[fo, fi, 0] * spec[fi] + gmap[fo, fi, 1] * swapped[fi]
            fsend[e, h, pl.ds(fo * 32, 32), :] = o
            total += jnp.sum(spec[fo] * o, axis=0, keepdims=True)
        gn_ref[h] = total

    def read_spec(ref):
        return [ref[pl.ds(f * 32, 32), :] for f in range(NF)]

    fsend[0] = spec_ref[...]
    pl.semaphore_wait(bar, NTILE - 1 + NF - 1)
    fstart(0, 0)
    fstart(0, 1)

    flat = jnp.concatenate([data_ref[c, h * 32:(h + 1) * 32, :] for h in range(2) for c in range(2)], 0).T
    for b in range(4):
        first, second = flat[b * 64:b * 64 + 32], flat[b * 64 + 32:b * 64 + 64]
        left = lanes((32, 128)) < 64
        r0_ref[0, b * 32:(b + 1) * 32, :] = jnp.where(left, first, pltpu.roll(second, 64, 1))
        r0_ref[1, b * 32:(b + 1) * 32, :] = jnp.where(left, pltpu.roll(first, 64, 1), second)

    loads[0].wait()

    @pl.loop(0, 2)
    def _(h):
        fwait(0, h)
        send_products(0, h, vt, frecv[0, h])

    loads[1].wait()
    setup_wide(ut, un)

    @pl.loop(0, 2)
    def _(h):
        r0_ref[h] = gather_products(0, h, un) - r0_ref[h]
        send_products(1, h, ut, r0_ref[h])

    setup_wide(vt, vn)
    setup_gram()

    @pl.loop(0, 2)
    def _(h):
        fsend[1, h] = gather_products(1, h, vn)
        fstart(1, h)

    @pl.loop(0, 2)
    def _(h):
        fwait(1, h)
        spec0[h] = frecv[1, h]
        mix(2, h, read_spec(spec0.at[h]))
        fstart(2, h)

    @pl.loop(0, 2)
    def _(h):
        fwait(2, h)
        send_products(2, h, vt, frecv[2, h])

    @pl.loop(0, 2)
    def _(h):
        im_ref[h] = gather_products(2, h, un)
        send_products(3, h, ut, im_ref[h])

    sum_start(0, gn_ref[0] + gn_ref[1], (im_ref[0], im_ref[1]))
    fsend[3, 0] = gather_products(3, 0, vn)
    fstart(3, 0)
    sum_middle(0)
    fsend[3, 1] = gather_products(3, 1, vn)
    fstart(3, 1)
    alpha0 = sum_end(0)

    @pl.loop(0, 2)
    def _(h):
        fwait(3, h)
        comb_ref[h] = spec0[h] - alpha0 * frecv[3, h]
        mix(4, h, read_spec(comb_ref.at[h]))
        fstart(4, h)

    @pl.loop(0, 2)
    def _(h):
        fwait(4, h)
        send_products(4, h, vt, frecv[4, h])

    for h in range(2):
        r0_ref[h] = r0_ref[h] - alpha0 * im_ref[h]

    @pl.loop(0, 2)
    def _(h):
        im_ref[h] = gather_products(4, h, un)

    sum_start(1, gn_ref[0] + gn_ref[1], (im_ref[0], im_ref[1]))

    @pl.loop(0, 5)
    def _(e):
        for h in range(2):
            sent(e, h)

    sum_middle(1)
    alpha1 = sum_end(1)
    for h in range(2):
        comb_ref[h] = alpha0 * spec0[h] + alpha1 * comb_ref[h]
    blocks = []
    p0, p1 = (r0_ref[h] - alpha1 * im_ref[h] for h in range(2))
    for b in range(4):
        left = lanes((32, 128)) < 64
        a0, a1 = p0[b * 32:(b + 1) * 32], p1[b * 32:(b + 1) * 32]
        blocks.append(jnp.where(left, a0, pltpu.roll(a1, 64, 1)))
        blocks.append(jnp.where(left, pltpu.roll(a0, 64, 1), a1))
    flat = jnp.concatenate(blocks, 0).T
    for h in range(2):
        for c in range(2):
            resid_ref[c, h * 32:(h + 1) * 32, :] = flat[(h * 2 + c) * 32:(h * 2 + c + 1) * 32]


def update_kernel(mute_ref, comb_ref, b3_ref, x_ref, o_ref):
    g = pl.program_id(0)
    n = x_ref.shape[1]
    b3 = b3_ref[...]
    t = lanes((NV, NT))
    quarter = even((4, 128))
    for i in range(n):
        m = g * n + i
        p0, p1 = (comb_ref[h, pl.ds(m, 4, stride=32), :] for h in range(2))
        re = jnp.where(quarter, p0, pltpu.roll(p1, 32, 1))
        im = jnp.where(quarter, pltpu.roll(p0, 96, 1), p1)
        hi, lo = split(jnp.concatenate([re, im], 0))
        hi, lo = hi.astype(F32), lo.astype(F32)
        lhs = jnp.concatenate([hi, lo, hi, jnp.zeros_like(hi)], 0)
        grad = dot(lhs.T.astype(BF16), b3)
        for s in range(2):
            part = jnp.where(t >= mute_ref[s * 32 + m], grad[s * 64:(s + 1) * 64], 0.0)
            o_ref[s, i] = x_ref[s, i] - part


def body(x_time, mute, ranks, right_factor_columns, u_rows, data):
    b = basis()
    bhi, blo = split(jnp.asarray(b))
    bb = jnp.concatenate([bhi, blo], 0)
    b3 = jnp.concatenate([bhi, bhi, blo, jnp.zeros_like(bhi)], 0)
    prod = np.zeros((NT, 128), np.float32)
    prod[:, :64] = (b[:, None, :] * b[None, :, :]).reshape(64, NT).T
    me = lax.axis_index("tile")
    place = np.array([(*(FIRST, SECOND)[j // 2][g], j % 2) for g in range(NG) for j in range(4)], np.int32)
    perm = (me // 8 + place[:, 0]) % 4 * 8 + (me // 2 % 4 + place[:, 1]) % 4 * 2 + (me % 2 + place[:, 2]) % 2
    vmem = pl.BlockSpec(memory_space=pltpu.VMEM)
    hbm = pl.BlockSpec(memory_space=pl.ANY)
    smem = pl.BlockSpec(memory_space=pltpu.SMEM)
    dma = pltpu.SemaphoreType.DMA
    tiles = jax.ShapeDtypeStruct((NG, 512, 512), BF16)
    spec, vt, ut = pl.pallas_call(
        setup_kernel,
        out_shape=(jax.ShapeDtypeStruct((2, 128, 128), F32), tiles, tiles),
        in_specs=[smem, smem, smem, hbm, hbm, hbm, vmem],
        out_specs=(vmem, hbm, hbm),
        scratch_shapes=[
            pltpu.VMEM((4096, 256), F32),
            pltpu.VMEM((2, 2, 256, NTILE * 64), F32),
            pltpu.VMEM((2, 2, NTILE * 64, 128), F32),
            pltpu.VMEM((2, NG, 512, 512), BF16),
            pltpu.SMEM((2, NTILE), jnp.int32),
            dma((5,)), dma((2, NG)),
        ],
        compiler_params=pltpu.CompilerParams(vmem_limit_bytes=ROOM),
        name="setup",
    )(me.reshape(1), perm.astype(jnp.int32), ranks[0], x_time.reshape(4096, 256), right_factor_columns[0, :, 0], u_rows[0, :, 0], bb)
    pairs = (2, 128, 128)
    comb, resid = pl.pallas_call(
        main_kernel,
        out_shape=(jax.ShapeDtypeStruct(pairs, F32), jax.ShapeDtypeStruct((2, NV, NB), F32)),
        in_specs=[smem, vmem, hbm, hbm, vmem, vmem],
        out_specs=(vmem, vmem),
        scratch_shapes=[
            pltpu.VMEM((NG, 512, 512), BF16),
            pltpu.VMEM((NG, 512, 512), BF16),
            pltpu.VMEM((NG, 512, 512), BF16),
            pltpu.VMEM((NG, 512, 512), BF16),
            pltpu.VMEM((5, 2, NTILE, 32, 128), F32),
            pltpu.VMEM((5, 2, NTILE, 32, 128), F32),
            pltpu.VMEM((5, *pairs), F32),
            pltpu.VMEM((5, *pairs), F32),
            pltpu.VMEM(pairs, F32),
            pltpu.VMEM((512, 128), BF16),
            pltpu.VMEM((512, 128), F32),
            pltpu.VMEM((BLK, NT), F32),
            pltpu.VMEM((NF, NF, 2, 32, 128), F32),
            pltpu.VMEM(pairs, F32),
            pltpu.VMEM(pairs, F32),
            pltpu.VMEM((2, 1, 128), F32),
            pltpu.VMEM((2, 8, 128), F32),
            pltpu.VMEM((2, NTILE, 8, 128), F32),
            pltpu.VMEM((2, 8, 128), F32),
            pltpu.VMEM((2, NF, 8, 128), F32),
            dma((2,)), dma((5, 2, NTILE)), dma((5, 2, NTILE)), dma((5, 2, NF)), dma((5, 2, NF)),
            dma((2, NTILE)), dma((2, NTILE)), dma((2, NF)), dma((2, NF)),
        ],
        compiler_params=pltpu.CompilerParams(collective_id=0, has_side_effects=True, vmem_limit_bytes=ROOM),
        name="descent",
    )(mute, spec, vt, ut, data[0].swapaxes(1, 2), jnp.asarray(prod))
    step = 8
    x_out = pl.pallas_call(
        update_kernel,
        grid=(32 // step,),
        out_shape=jax.ShapeDtypeStruct((2, 32, NV, NT), F32),
        in_specs=[
            smem, vmem, vmem,
            pl.BlockSpec((2, step, NV, NT), lambda i: (0, i, 0, 0)),
        ],
        out_specs=pl.BlockSpec((2, step, NV, NT), lambda i: (0, i, 0, 0)),
        compiler_params=pltpu.CompilerParams(vmem_limit_bytes=ROOM),
        name="update",
    )(mute, comb, b3, x_time.reshape(2, 32, NV, NT))
    return x_out.reshape(BLK, NV, NT), resid.swapaxes(1, 2)[None]


def solution(mesh):
    in_specs = (
        P(("tile", "freq"), None, None),
        P(("tile", "freq")),
        P("freq", None, None),
        P("freq", None, "tile", None, None),
        P("freq", None, "tile", None, None),
        P("freq", None, "tile", None),
    )
    out_specs = (P(("tile", "freq"), None, None), P("freq", None, "tile", None))
    return jax.shard_map(body, mesh=mesh, in_specs=in_specs, out_specs=out_specs, check_vma=False)
```

```python
import jax
import jax.numpy as jnp
import numpy as np
from jax import lax
from jax.experimental import pallas as pl
from jax.experimental.pallas import tpu as pltpu
from jax.sharding import PartitionSpec as P

FLO = 16
MESH = pl.DeviceIdType.MESH
F32, BF16 = jnp.float32, jnp.bfloat16
NF, NTILE, NB, NV, NT, BLK = 4, 32, 256, 64, 256, 64
NG = 8
STEP = 4
ROOM = 60 << 20

FIRST = ((0, 0), (2, 1), (1, 2), (1, 1), (1, 3), (2, 0), (1, 0), (0, 1))
SECOND = ((2, 2), (2, 3), (3, 2), (3, 3), (3, 1), (0, 2), (3, 0), (0, 3))
OWN = 0


def basis():
    steps = np.arange(NT)
    freqs = FLO + np.arange(NF)
    angle = (freqs[:, None] * steps[None, :] % NT).astype(np.float32) * np.float32(2.0 * np.pi / NT)
    return np.concatenate([np.cos(angle), -np.sin(angle)]).astype(np.float32)


def split(a):
    hi = a.astype(BF16)
    return hi, (a - hi.astype(F32)).astype(BF16)


def dot(a, b, dims=((1,), (0,))):
    return lax.dot_general(a, b, (dims, ((), ())), preferred_element_type=F32)


def lanes(shape):
    return lax.broadcasted_iota(jnp.int32, shape, 1)


def even(shape):
    return lax.rem(lanes(shape), 64) < 32


def swap(p):
    return jnp.where(even(p.shape), pltpu.roll(p, 96, 1), pltpu.roll(p, 32, 1))


def rhs(p, sign):
    left = lanes(p.shape) < 64
    s = swap(p)
    out = []
    for q in (p, jnp.where(even(p.shape), sign * s, -sign * s)):
        hi = q.astype(BF16).astype(F32)
        lo = q - hi
        out.append(jnp.where(left, hi, pltpu.roll(lo, 64, 1)).astype(BF16))
        out.append(jnp.where(left, pltpu.roll(hi, 64, 1), lo).astype(BF16))
    return jnp.concatenate(out, 0)


def pack(o):
    s = o[:256] + o[256:]
    s = s + pltpu.roll(s, 64, 1)
    return jnp.where(lanes((128, 128)) < 64, s[:128], s[128:])


def tile_at(me, g, j):
    table, dc = (FIRST, SECOND)[j // 2], j % 2
    dz, dy = jnp.int32(table[0][0]), jnp.int32(table[0][1])
    for i in range(1, NG):
        dz, dy = jnp.where(g == i, table[i][0], dz), jnp.where(g == i, table[i][1], dy)
    return lax.rem(me // 8 + dz, 4) * 8 + lax.rem(lax.rem(me // 2, 4) + dy, 4) * 2 + lax.rem(lax.rem(me, 2) + dc, 2)


def setup_kernel(ranks_ref, v_hbm, u_hbm, vt_hbm, ut_hbm, raw, tall, packed, offs, ld_sem, st_sem):
    me = lax.axis_index("tile")
    loads = []
    for m, hbm in enumerate((v_hbm, u_hbm)):
        for c in range(2):
            loads.append(pltpu.make_async_copy(hbm.at[c], raw.at[m, c], ld_sem.at[m * 2 + c]))
    for cp in loads:
        cp.start()

    def offsets(m, rank_at):
        def one(i, off):
            offs[m, i] = off
            return off + rank_at(i)

        lax.fori_loop(0, NTILE, one, jnp.int32(0))

    ranks_at = (lambda i: ranks_ref[i, me]), (lambda j: ranks_ref[me, j])
    offsets(0, ranks_at[0])
    offsets(1, ranks_at[1])

    def flip(m):
        for c in range(2):
            loads[m * 2 + c].wait()

            @pl.loop(0, 16)
            def _(b):
                cols = pl.ds(pl.multiple_of(b * 128, 128), 128)
                order = [64 * i for i in range(4)] + [64 * i + 32 for i in range(4)]
                turned = jnp.concatenate([raw[m, c, i:i + 32, cols] for i in order], 0).T
                tall[c, 0, cols, :] = turned[:, :128]
                tall[c, 1, cols, :] = turned[:, 128:]

    def store(m, g):
        return pltpu.make_async_copy(packed.at[m, g], (vt_hbm, ut_hbm)[m].at[g], st_sem.at[m, g])

    def pad(m):
        @pl.loop(0, NG)
        def _(g):
            for j in range(4):
                tile = tile_at(me, g, j)
                k = ranks_at[m](tile)
                off = offs[m, tile]
                for c in range(2):
                    piece = jnp.concatenate([tall[c, h, pl.ds(off, 64), :] for h in range(2)], 1)
                    slot = lax.broadcasted_iota(jnp.int32, (64, NB), 0)
                    for n, part in enumerate(split(jnp.where(slot < k, piece, 0.0))):
                        for h in range(2):
                            at = n * 256 + h * 128 + j * 32
                            packed[m, g, at:at + 32, c * 256:(c + 1) * 256] = part[h * 32:(h + 1) * 32]
            store(m, g).start()

    for m in range(2):
        flip(m)
        pad(m)
    for m in range(2):
        @pl.loop(0, NG)
        def _(g):
            store(m, g).wait()


def main_kernel(
    mute_ref, x_hbm, vt_hbm, ut_hbm, data_ref, bb_ref, prod_ref,
    comb_ref, resid_ref,
    x_buf, vt, vn, ut, un, wbuf, zbuf, fsend, frecv, spec0, right, acc,
    keep_ref, gmap, r0_ref, im_ref, gn_ref, sc_send, sc_recv, sc2_send, sc2_recv,
    ld_sem, ts_sem, tr_sem, fs_sem, fr_sem, ss_sem, sr_sem, s2s_sem, s2r_sem,
):
    me = lax.axis_index("tile")
    fme = lax.axis_index("freq")

    loads = [
        pltpu.make_async_copy(x_hbm, x_buf, ld_sem.at[2]),
        pltpu.make_async_copy(vt_hbm, vt, ld_sem.at[0]),
        pltpu.make_async_copy(ut_hbm, ut, ld_sem.at[1]),
    ]
    for cp in loads:
        cp.start()

    bar = pltpu.get_barrier_semaphore()

    @pl.loop(1, NTILE)
    def _(d):
        pl.semaphore_signal(bar, inc=1, device_id={"tile": lax.rem(me + d, NTILE)}, device_id_type=MESH)

    for d in range(1, NF):
        pl.semaphore_signal(bar, inc=1, device_id={"freq": lax.rem(fme + d, NF)}, device_id_type=MESH)

    def setup_wide(t_ref, n_ref):
        @pl.loop(0, NG)
        def _(g):
            for p in range(2):
                for c in range(2):
                    n_ref[g, p * 256:(p + 1) * 256, c * 256:(c + 1) * 256] = (
                        t_ref[g, p * 256:(p + 1) * 256, c * 256:(c + 1) * 256].T)

    def fcopy(e, h, peer, at):
        return pltpu.make_async_remote_copy(
            src_ref=fsend.at[e, h, pl.ds(pl.multiple_of(peer * 32, 32), 32)],
            dst_ref=frecv.at[e, h, pl.ds(pl.multiple_of(at * 32, 32), 32)],
            send_sem=fs_sem.at[e, h, peer], recv_sem=fr_sem.at[e, h, at],
            device_id={"freq": peer}, device_id_type=MESH)

    def fstart(e, h):
        for d in (2, 1, 3):
            fcopy(e, h, lax.rem(fme + d, NF), fme).start()

    def fwait(e, h):
        for d in range(1, NF):
            peer = lax.rem(fme + d, NF)
            fcopy(e, h, peer, peer).wait()
        own = pl.ds(pl.multiple_of(fme * 32, 32), 32)
        frecv[e, h, own, :] = fsend[e, h, own, :]

    def tcopy(e, h, g, j):
        half, dc = j // 2, j % 2
        peer = tile_at(me, g, j)
        same = jnp.logical_or(g == 0, g == 5)
        slot = g * 4 + jnp.where(same, half, 1 - half) * 2 + dc
        return pltpu.make_async_remote_copy(
            src_ref=wbuf.at[e, h, g * 4 + j], dst_ref=zbuf.at[e, h, slot],
            send_sem=ts_sem.at[e, h], recv_sem=tr_sem.at[e, h, g // STEP],
            device_id={"tile": peer}, device_id_type=MESH)

    def arrivals(e, h, k):
        slots = pl.ds(max(k * STEP * 4, 1), STEP * 4 - (k == 0))
        return pltpu.make_async_remote_copy(
            src_ref=wbuf.at[e, h, slots], dst_ref=zbuf.at[e, h, slots],
            send_sem=ts_sem.at[e, h], recv_sem=tr_sem.at[e, h, k],
            device_id={"tile": lax.rem(me + 1, NTILE)}, device_id_type=MESH)

    def send_products(e, h, t_ref, p, sign=1.0):
        right[...] = rhs(p, sign)

        @pl.loop(0, NG // STEP)
        def _(k):
            o = dot(t_ref[pl.ds(k * STEP, STEP)].reshape(STEP * 512, 512), right[...])
            for i in range(STEP):
                wbuf[e, h, pl.ds((k * STEP + i) * 4, 4)] = pack(o[i * 512:(i + 1) * 512]).reshape(4, 32, 128)
            for i in range(STEP):
                for j in range(4):
                    if i or j != OWN:
                        tcopy(e, h, k * STEP + i, j).start()
                    else:
                        @pl.when(k > 0)
                        def _():
                            tcopy(e, h, k * STEP, OWN).start()

    def gather_part(e, h, n_ref, k):
        arrivals(e, h, k).wait_recv()
        if k == 0:
            zbuf[e, h, OWN] = wbuf[e, h, OWN]
        total = None
        for g in range(k * STEP, (k + 1) * STEP):
            z = zbuf[e, h, g * 4:g * 4 + 4].reshape(128, 128)
            o = dot(n_ref[g], rhs(z, -1.0))
            total = o if total is None else total + o
        if k == 0:
            acc[...] = total
        else:
            acc[...] += total

    def gather_products(e, h, n_ref):
        for k in range(NG // STEP):
            gather_part(e, h, n_ref, k)
        return pack(acc[...])

    def sent(e, h):
        slots = pl.ds(1, NTILE - 1)
        pltpu.make_async_remote_copy(
            src_ref=wbuf.at[e, h, slots], dst_ref=zbuf.at[e, h, slots],
            send_sem=ts_sem.at[e, h], recv_sem=tr_sem.at[e, h, 0],
            device_id={"tile": lax.rem(me + 1, NTILE)}, device_id_type=MESH).wait_send()

    def scopy(n, d):
        return pltpu.make_async_remote_copy(
            src_ref=sc_send.at[n], dst_ref=sc_recv.at[n, d],
            send_sem=ss_sem.at[n], recv_sem=sr_sem.at[n],
            device_id={"tile": lax.rem(me + d, NTILE)}, device_id_type=MESH)

    def s2copy(n, peer, at):
        return pltpu.make_async_remote_copy(
            src_ref=sc2_send.at[n], dst_ref=sc2_recv.at[n, at],
            send_sem=s2s_sem.at[n, peer], recv_sem=s2r_sem.at[n, at],
            device_id={"freq": peer}, device_id_type=MESH)

    def sum_start(n, gn, im):
        row = lax.broadcasted_iota(jnp.int32, (8, 128), 0)
        inn = sum(jnp.sum(i * i, axis=0, keepdims=True) for i in im)
        sc_send[n] = jnp.where(row == 0, gn, jnp.where(row == 1, inn, 0.0))

        @pl.loop(1, NTILE)
        def _(d):
            scopy(n, d).start()

    def sum_middle(n):
        rest = sc_recv.at[n, pl.ds(1, NTILE - 1)]
        pltpu.make_async_remote_copy(
            src_ref=rest, dst_ref=rest, send_sem=ss_sem.at[n], recv_sem=sr_sem.at[n],
            device_id={"tile": lax.rem(me + 1, NTILE)}, device_id_type=MESH).wait()
        sc_recv[n, 0] = sc_send[n]
        part = jnp.sum(sc_recv[n], axis=0)
        sc2_send[n] = part
        for d in range(1, NF):
            s2copy(n, lax.rem(fme + d, NF), fme).start()

    def sum_end(n):
        for d in range(1, NF):
            peer = lax.rem(fme + d, NF)
            s2copy(n, peer, peer).wait()
        sc2_recv[n, fme] = sc2_send[n]
        both = jnp.sum(jnp.sum(sc2_recv[n], axis=0), axis=1, keepdims=True)
        return both[0:1] / both[1:2]

    def setup_gram():
        @pl.loop(0, BLK)
        def _(r):
            t = lanes((1, NT))
            keep_ref[pl.ds(r, 1), :] = (t >= mute_ref[r]).astype(F32)

        gram = jnp.dot(keep_ref[...], prod_ref[...], precision=lax.Precision.HIGHEST, preferred_element_type=F32)
        lane = lanes((32, 128))
        left, real = lane < 64, even((32, 128))

        def col(a, b):
            i = a * 8 + b
            return jnp.where(left, gram[:32, i:i + 1], gram[32:, i:i + 1])

        for fo in range(NF):
            for fi in range(NF):
                gmap[fo, fi, 0] = jnp.where(real, col(fo, fi), col(4 + fo, 4 + fi))
                gmap[fo, fi, 1] = jnp.where(real, col(fo, 4 + fi), col(4 + fo, fi))

    def mix(e, h, spec):
        swapped = [swap(s) for s in spec]
        total = jnp.zeros((1, 128), F32)
        for fo in range(NF):
            o = jnp.zeros((32, 128), F32)
            for fi in range(NF):
                o += gmap[fo, fi, 0] * spec[fi] + gmap[fo, fi, 1] * swapped[fi]
            fsend[e, h, pl.ds(fo * 32, 32), :] = o
            total += jnp.sum(spec[fo] * o, axis=0, keepdims=True)
        gn_ref[h] = total

    def read_spec(ref):
        return [ref[pl.ds(f * 32, 32), :] for f in range(NF)]

    loads[0].wait()
    bb = bb_ref[...]
    quarter = even((4, 128))

    @pl.loop(0, BLK // 4)
    def _(k):
        low = pl.multiple_of(k * 128, 128)
        a, b = x_buf[pl.ds(low, 128), :], x_buf[pl.ds(BLK * 32 + low, 128), :]
        hi, lo = split(jnp.concatenate([a[:64], b[:64], a[64:], b[64:]], 0))
        o1 = dot(bb, hi, ((1,), (1,)))
        o2 = dot(bb, lo, ((1,), (1,)))
        o = o1[:8] + o1[8:] + o2[:8]
        for i in range(2):
            re, im = o[:4, i * 128:(i + 1) * 128], o[4:, i * 128:(i + 1) * 128]
            rows = pl.ds(k * 2 + i, 4, stride=32)
            fsend[0, 0, rows, :] = jnp.where(quarter, re, pltpu.roll(im, 32, 1))
            fsend[0, 1, rows, :] = jnp.where(quarter, pltpu.roll(re, 96, 1), im)

    pl.semaphore_wait(bar, NTILE - 1 + NF - 1)
    fstart(0, 0)
    fstart(0, 1)

    flat = jnp.concatenate([data_ref[c, h * 32:(h + 1) * 32, :] for h in range(2) for c in range(2)], 0).T
    for b in range(4):
        first, second = flat[b * 64:b * 64 + 32], flat[b * 64 + 32:b * 64 + 64]
        left = lanes((32, 128)) < 64
        r0_ref[0, b * 32:(b + 1) * 32, :] = jnp.where(left, first, pltpu.roll(second, 64, 1))
        r0_ref[1, b * 32:(b + 1) * 32, :] = jnp.where(left, pltpu.roll(first, 64, 1), second)

    loads[1].wait()

    @pl.loop(0, 2)
    def _(h):
        fwait(0, h)
        send_products(0, h, vt, frecv[0, h])

    loads[2].wait()
    setup_wide(ut, un)

    @pl.loop(0, 2)
    def _(h):
        r0_ref[h] = gather_products(0, h, un) - r0_ref[h]
        send_products(1, h, ut, r0_ref[h])

    setup_wide(vt, vn)
    setup_gram()

    def adjoint_and_back(e, use, alpha):
        k = NG // STEP - 1
        fsend[e, 0] = gather_products(e, 0, vn)
        fstart(e, 0)
        for i in range(k):
            gather_part(e, 1, vn, i)
        a = alpha()
        fwait(e, 0)
        use(0, a)
        fstart(e + 1, 0)
        gather_part(e, 1, vn, k)
        fsend[e, 1] = pack(acc[...])
        fstart(e, 1)
        fwait(e + 1, 0)
        send_products(e + 1, 0, vt, frecv[e + 1, 0])
        fwait(e, 1)
        use(1, a)
        fstart(e + 1, 1)
        fwait(e + 1, 1)
        send_products(e + 1, 1, vt, frecv[e + 1, 1])
        return a

    def first_use(h, a):
        spec0[h] = frecv[1, h]
        mix(2, h, read_spec(spec0.at[h]))

    adjoint_and_back(1, first_use, lambda: None)

    im_ref[0] = gather_products(2, 0, un)
    send_products(3, 0, ut, im_ref[0])
    im_ref[1] = gather_products(2, 1, un)
    sum_start(0, gn_ref[0] + gn_ref[1], (im_ref[0], im_ref[1]))
    send_products(3, 1, ut, im_ref[1])
    sum_middle(0)

    def second_use(h, a):
        comb_ref[h] = spec0[h] - a * frecv[3, h]
        mix(4, h, read_spec(comb_ref.at[h]))

    alpha0 = adjoint_and_back(3, second_use, lambda: sum_end(0))

    for h in range(2):
        r0_ref[h] = r0_ref[h] - alpha0 * im_ref[h]

    @pl.loop(0, 2)
    def _(h):
        im_ref[h] = gather_products(4, h, un)

    sum_start(1, gn_ref[0] + gn_ref[1], (im_ref[0], im_ref[1]))

    @pl.loop(0, 5)
    def _(e):
        for h in range(2):
            sent(e, h)

    sum_middle(1)
    alpha1 = sum_end(1)
    for h in range(2):
        comb_ref[h] = alpha0 * spec0[h] + alpha1 * comb_ref[h]
    blocks = []
    p0, p1 = (r0_ref[h] - alpha1 * im_ref[h] for h in range(2))
    for b in range(4):
        left = lanes((32, 128)) < 64
        a0, a1 = p0[b * 32:(b + 1) * 32], p1[b * 32:(b + 1) * 32]
        blocks.append(jnp.where(left, a0, pltpu.roll(a1, 64, 1)))
        blocks.append(jnp.where(left, pltpu.roll(a0, 64, 1), a1))
    flat = jnp.concatenate(blocks, 0).T
    for h in range(2):
        for c in range(2):
            resid_ref[c, h * 32:(h + 1) * 32, :] = flat[(h * 2 + c) * 32:(h * 2 + c + 1) * 32]


def update_kernel(mute_ref, comb_ref, b3_ref, x_ref, o_ref):
    g = pl.program_id(0)
    n = x_ref.shape[1]
    b3 = b3_ref[...]
    t = lanes((NV, NT))
    quarter = even((4, 128))
    for i in range(n):
        m = g * n + i
        p0, p1 = (comb_ref[h, pl.ds(m, 4, stride=32), :] for h in range(2))
        re = jnp.where(quarter, p0, pltpu.roll(p1, 32, 1))
        im = jnp.where(quarter, pltpu.roll(p0, 96, 1), p1)
        hi, lo = split(jnp.concatenate([re, im], 0))
        hi, lo = hi.astype(F32), lo.astype(F32)
        lhs = jnp.concatenate([hi, lo, hi, jnp.zeros_like(hi)], 0)
        grad = dot(lhs.T.astype(BF16), b3)
        for s in range(2):
            part = jnp.where(t >= mute_ref[s * 32 + m], grad[s * 64:(s + 1) * 64], 0.0)
            o_ref[s, i] = x_ref[s, i] - part


def body(x_time, mute, ranks, right_factor_columns, u_rows, data):
    b = basis()
    bhi, blo = split(jnp.asarray(b))
    bb = jnp.concatenate([bhi, blo], 0)
    b3 = jnp.concatenate([bhi, bhi, blo, jnp.zeros_like(bhi)], 0)
    prod = np.zeros((NT, 128), np.float32)
    prod[:, :64] = (b[:, None, :] * b[None, :, :]).reshape(64, NT).T
    vmem = pl.BlockSpec(memory_space=pltpu.VMEM)
    hbm = pl.BlockSpec(memory_space=pl.ANY)
    smem = pl.BlockSpec(memory_space=pltpu.SMEM)
    dma = pltpu.SemaphoreType.DMA
    tiles = jax.ShapeDtypeStruct((NG, 512, 512), BF16)
    vt, ut = pl.pallas_call(
        setup_kernel,
        out_shape=(tiles, tiles),
        in_specs=[smem, hbm, hbm],
        out_specs=(hbm, hbm),
        scratch_shapes=[
            pltpu.VMEM((2, 2, 256, NTILE * 64), F32),
            pltpu.VMEM((2, 2, NTILE * 64, 128), F32),
            pltpu.VMEM((2, NG, 512, 512), BF16),
            pltpu.SMEM((2, NTILE), jnp.int32),
            dma((4,)), dma((2, NG)),
        ],
        compiler_params=pltpu.CompilerParams(vmem_limit_bytes=ROOM),
        name="setup",
    )(ranks[0], right_factor_columns[0, :, 0], u_rows[0, :, 0])
    pairs = (2, 128, 128)
    comb, resid = pl.pallas_call(
        main_kernel,
        out_shape=(jax.ShapeDtypeStruct(pairs, F32), jax.ShapeDtypeStruct((2, NV, NB), F32)),
        in_specs=[smem, hbm, hbm, hbm, vmem, vmem, vmem],
        out_specs=(vmem, vmem),
        scratch_shapes=[
            pltpu.VMEM((4096, 256), F32),
            pltpu.VMEM((NG, 512, 512), BF16),
            pltpu.VMEM((NG, 512, 512), BF16),
            pltpu.VMEM((NG, 512, 512), BF16),
            pltpu.VMEM((NG, 512, 512), BF16),
            pltpu.VMEM((5, 2, NTILE, 32, 128), F32),
            pltpu.VMEM((5, 2, NTILE, 32, 128), F32),
            pltpu.VMEM((5, *pairs), F32),
            pltpu.VMEM((5, *pairs), F32),
            pltpu.VMEM(pairs, F32),
            pltpu.VMEM((512, 128), BF16),
            pltpu.VMEM((512, 128), F32),
            pltpu.VMEM((BLK, NT), F32),
            pltpu.VMEM((NF, NF, 2, 32, 128), F32),
            pltpu.VMEM(pairs, F32),
            pltpu.VMEM(pairs, F32),
            pltpu.VMEM((2, 1, 128), F32),
            pltpu.VMEM((2, 8, 128), F32),
            pltpu.VMEM((2, NTILE, 8, 128), F32),
            pltpu.VMEM((2, 8, 128), F32),
            pltpu.VMEM((2, NF, 8, 128), F32),
            dma((3,)), dma((5, 2)), dma((5, 2, NG // STEP)), dma((5, 2, NF)), dma((5, 2, NF)),
            dma((2,)), dma((2,)), dma((2, NF)), dma((2, NF)),
        ],
        compiler_params=pltpu.CompilerParams(collective_id=0, has_side_effects=True, vmem_limit_bytes=ROOM),
        name="descent",
    )(mute, x_time.reshape(4096, 256), vt, ut, data[0].swapaxes(1, 2), bb, jnp.asarray(prod))
    step = 16
    x_out = pl.pallas_call(
        update_kernel,
        grid=(32 // step,),
        out_shape=jax.ShapeDtypeStruct((2, 32, NV, NT), F32),
        in_specs=[
            smem, vmem, vmem,
            pl.BlockSpec((2, step, NV, NT), lambda i: (0, i, 0, 0)),
        ],
        out_specs=pl.BlockSpec((2, step, NV, NT), lambda i: (0, i, 0, 0)),
        compiler_params=pltpu.CompilerParams(vmem_limit_bytes=ROOM),
        name="update",
    )(mute, comb, b3, x_time.reshape(2, 32, NV, NT))
    return x_out.reshape(BLK, NV, NT), resid.swapaxes(1, 2)[None]


def solution(mesh):
    in_specs = (
        P(("tile", "freq"), None, None),
        P(("tile", "freq")),
        P("freq", None, None),
        P("freq", None, "tile", None, None),
        P("freq", None, "tile", None, None),
        P("freq", None, "tile", None),
    )
    out_specs = (P(("tile", "freq"), None, None), P("freq", None, "tile", None))
    return jax.shard_map(body, mesh=mesh, in_specs=in_specs, out_specs=out_specs, check_vma=False)
```

```python
import jax
import jax.numpy as jnp
import numpy as np
from jax import lax
from jax.experimental import pallas as pl
from jax.experimental.pallas import tpu as pltpu
from jax.sharding import PartitionSpec as P

FLO = 16
MESH = pl.DeviceIdType.MESH
F32, BF16 = jnp.float32, jnp.bfloat16
NF, NTILE, NB, NV, NT, BLK = 4, 32, 256, 64, 256, 64
NG = 8
STEP = 4
NPLANE = NF * (NTILE // 8)
ROOM = 60 << 20

FIRST = ((0, 0), (2, 1), (1, 2), (1, 1), (1, 3), (2, 0), (1, 0), (0, 1))
SECOND = ((2, 2), (2, 3), (3, 2), (3, 3), (3, 1), (0, 2), (3, 0), (0, 3))
OWN = 0


def basis():
    steps = np.arange(NT)
    freqs = FLO + np.arange(NF)
    angle = (freqs[:, None] * steps[None, :] % NT).astype(np.float32) * np.float32(2.0 * np.pi / NT)
    return np.concatenate([np.cos(angle), -np.sin(angle)]).astype(np.float32)


def split(a):
    hi = a.astype(BF16)
    return hi, (a - hi.astype(F32)).astype(BF16)


def dot(a, b, dims=((1,), (0,))):
    return lax.dot_general(a, b, (dims, ((), ())), preferred_element_type=F32)


def lanes(shape):
    return lax.broadcasted_iota(jnp.int32, shape, 1)


def even(shape):
    return lax.rem(lanes(shape), 64) < 32


def swap(p):
    return jnp.where(even(p.shape), pltpu.roll(p, 96, 1), pltpu.roll(p, 32, 1))


def rhs(p, sign):
    left = lanes(p.shape) < 64
    s = swap(p)
    out = []
    for q in (p, jnp.where(even(p.shape), sign * s, -sign * s)):
        hi = q.astype(BF16).astype(F32)
        lo = q - hi
        out.append(jnp.where(left, hi, pltpu.roll(lo, 64, 1)).astype(BF16))
        out.append(jnp.where(left, pltpu.roll(hi, 64, 1), lo).astype(BF16))
    return jnp.concatenate(out, 0)


def pack(o):
    s = o[:256] + o[256:]
    s = s + pltpu.roll(s, 64, 1)
    return jnp.where(lanes((128, 128)) < 64, s[:128], s[128:])


def tile_at(me, g, j):
    table, dc = (FIRST, SECOND)[j // 2], j % 2
    if isinstance(g, int):
        dz, dy = table[g]
    else:
        dz, dy = jnp.int32(table[0][0]), jnp.int32(table[0][1])
        for i in range(1, NG):
            dz, dy = jnp.where(g == i, table[i][0], dz), jnp.where(g == i, table[i][1], dy)
    return lax.rem(me // 8 + dz, 4) * 8 + lax.rem(lax.rem(me // 2, 4) + dy, 4) * 2 + lax.rem(lax.rem(me, 2) + dc, 2)


def setup_kernel(ranks_ref, v_hbm, u_hbm, vt_hbm, ut_hbm, raw, tall, packed, offs, ld_sem, st_sem):
    me = lax.axis_index("tile")
    loads = []
    for m, hbm in enumerate((v_hbm, u_hbm)):
        for c in range(2):
            loads.append(pltpu.make_async_copy(hbm.at[c], raw.at[m, c], ld_sem.at[m * 2 + c]))
    for cp in loads:
        cp.start()

    def offsets(m, rank_at):
        def one(i, off):
            offs[m, i] = off
            return off + rank_at(i)

        lax.fori_loop(0, NTILE, one, jnp.int32(0))

    ranks_at = (lambda i: ranks_ref[i, me]), (lambda j: ranks_ref[me, j])
    offsets(0, ranks_at[0])
    offsets(1, ranks_at[1])

    order = [64 * i for i in range(4)] + [64 * i + 32 for i in range(4)]

    def flip(m, n):
        c, cols = n // 16, pl.ds(pl.multiple_of(lax.rem(n, 16) * 128, 128), 128)
        turned = jnp.concatenate([raw[m, c, i:i + 32, cols] for i in order], 0).T
        tall[m, c, 0, cols, :] = turned[:, :128]
        tall[m, c, 1, cols, :] = turned[:, 128:]

    def store(m, g):
        return pltpu.make_async_copy(packed.at[m, g], (vt_hbm, ut_hbm)[m].at[g], st_sem.at[m, g])

    def pad(m, g):
        for j in range(4):
            tile = tile_at(me, g, j)
            k = ranks_at[m](tile)
            off = offs[m, tile]
            for c in range(2):
                piece = jnp.concatenate([tall[m, c, h, pl.ds(off, 64), :] for h in range(2)], 1)
                slot = lax.broadcasted_iota(jnp.int32, (64, NB), 0)
                for n, part in enumerate(split(jnp.where(slot < k, piece, 0.0))):
                    for h in range(2):
                        at = n * 256 + h * 128 + j * 32
                        packed[m, g, at:at + 32, c * 256:(c + 1) * 256] = part[h * 32:(h + 1) * 32]

    for c in range(2):
        loads[c].wait()

        @pl.loop(0, NTILE // 4)
        def _(b):
            for i in range(2):
                flip(0, c * 16 + b * 2 + i)

    loads[2].wait()
    loads[3].wait()

    @pl.loop(0, NG)
    def _(g):
        for i in range(4):
            flip(1, g * 4 + i)
        pad(0, g)
        store(0, g).start()

    @pl.loop(0, NG)
    def _(g):
        pad(1, g)
        store(1, g).start()

    for m in range(2):
        @pl.loop(0, NG)
        def _(g):
            store(m, g).wait()


def main_kernel(
    mute_ref, x_hbm, vt_hbm, ut_hbm, data_ref, bb_ref, prod_ref,
    comb_ref, resid_ref,
    x_buf, vt, vn, ut, un, wbuf, zbuf, fsend, frecv, spec0, right, acc,
    keep_ref, gmap, r0_ref, im_ref, gn_ref, sc_send, sc_recv, sc2_send, sc2_recv,
    ld_sem, ts_sem, tr_sem, fs_sem, fr_sem, ss_sem, sr_sem, s2s_sem, s2r_sem,
):
    me = lax.axis_index("tile")
    fme = lax.axis_index("freq")

    loads = [
        pltpu.make_async_copy(x_hbm, x_buf, ld_sem.at[2]),
        pltpu.make_async_copy(vt_hbm, vt, ld_sem.at[0]),
        pltpu.make_async_copy(ut_hbm, ut, ld_sem.at[1]),
    ]
    for cp in loads:
        cp.start()

    bar = pltpu.get_barrier_semaphore()

    @pl.loop(1, NTILE)
    def _(d):
        pl.semaphore_signal(bar, inc=1, device_id={"tile": lax.rem(me + d, NTILE)}, device_id_type=MESH)

    def plane_peer(d):
        w = lax.rem(me // 8 * NF + fme + d, NPLANE)
        return {"freq": lax.rem(w, NF), "tile": w // NF * 8 + lax.rem(me, 8)}

    met = 0
    for df in range(1, NF):
        for dz in range(NTILE // 8):
            peer = {"freq": lax.rem(fme + df, NF), "tile": lax.rem(me + 8 * dz, NTILE)}
            pl.semaphore_signal(bar, inc=1, device_id=peer, device_id_type=MESH)
            met += 1

    def setup_wide(t_ref, n_ref):
        @pl.loop(0, NG)
        def _(g):
            for p in range(2):
                for c in range(2):
                    n_ref[g, p * 256:(p + 1) * 256, c * 256:(c + 1) * 256] = (
                        t_ref[g, p * 256:(p + 1) * 256, c * 256:(c + 1) * 256].T)

    def fcopy(e, h, peer, at):
        return pltpu.make_async_remote_copy(
            src_ref=fsend.at[e, h, pl.ds(pl.multiple_of(peer * 32, 32), 32)],
            dst_ref=frecv.at[e, h, pl.ds(pl.multiple_of(at * 32, 32), 32)],
            send_sem=fs_sem.at[e, h, peer], recv_sem=fr_sem.at[e, h, at],
            device_id={"freq": peer}, device_id_type=MESH)

    def fstart(e, h):
        for d in (2, 1, 3):
            fcopy(e, h, lax.rem(fme + d, NF), fme).start()

    def fwait(e, h):
        for d in range(1, NF):
            peer = lax.rem(fme + d, NF)
            fcopy(e, h, peer, peer).wait()
        own = pl.ds(pl.multiple_of(fme * 32, 32), 32)
        frecv[e, h, own, :] = fsend[e, h, own, :]

    def tcopy(e, h, g, j):
        half, dc = j // 2, j % 2
        peer = tile_at(me, g, j)
        slot = g * 4 + (half if g in (0, 5) else 1 - half) * 2 + dc
        return pltpu.make_async_remote_copy(
            src_ref=wbuf.at[e, h, g * 4 + j], dst_ref=zbuf.at[e, h, slot],
            send_sem=ts_sem.at[e, h], recv_sem=tr_sem.at[e, h, g // STEP],
            device_id={"tile": peer}, device_id_type=MESH)

    def arrivals(e, h, k):
        slots = pl.ds(max(k * STEP * 4, 1), STEP * 4 - (k == 0))
        return pltpu.make_async_remote_copy(
            src_ref=wbuf.at[e, h, slots], dst_ref=zbuf.at[e, h, slots],
            send_sem=ts_sem.at[e, h], recv_sem=tr_sem.at[e, h, k],
            device_id={"tile": lax.rem(me + 1, NTILE)}, device_id_type=MESH)

    def send_part(e, h, t_ref, k):
        o = dot(t_ref[k * STEP:(k + 1) * STEP].reshape(STEP * 512, 512), right[...])
        for i in range(STEP):
            g = k * STEP + i
            wbuf[e, h, g * 4:g * 4 + 4] = pack(o[i * 512:(i + 1) * 512]).reshape(4, 32, 128)
        for i in range(STEP):
            for j in range(4):
                if k or i or j != OWN:
                    tcopy(e, h, k * STEP + i, j).start()

    def send_products(e, h, t_ref, p):
        right[...] = rhs(p, 1.0)
        for k in range(NG // STEP):
            send_part(e, h, t_ref, k)

    def gather_part(e, h, n_ref, k):
        arrivals(e, h, k).wait_recv()
        if k == 0:
            zbuf[e, h, OWN] = wbuf[e, h, OWN]
        total = None
        for g in range(k * STEP, (k + 1) * STEP):
            z = zbuf[e, h, g * 4:g * 4 + 4].reshape(128, 128)
            o = dot(n_ref[g], rhs(z, -1.0))
            total = o if total is None else total + o
        if k == 0:
            acc[...] = total
        else:
            acc[...] += total

    def gather_products(e, h, n_ref):
        for k in range(NG // STEP):
            gather_part(e, h, n_ref, k)
        return pack(acc[...])

    def sent(e, h):
        slots = pl.ds(1, NTILE - 1)
        pltpu.make_async_remote_copy(
            src_ref=wbuf.at[e, h, slots], dst_ref=zbuf.at[e, h, slots],
            send_sem=ts_sem.at[e, h], recv_sem=tr_sem.at[e, h, 0],
            device_id={"tile": lax.rem(me + 1, NTILE)}, device_id_type=MESH).wait_send()

    def scopy(n, d):
        return pltpu.make_async_remote_copy(
            src_ref=sc_send.at[n], dst_ref=sc_recv.at[n, d],
            send_sem=ss_sem.at[n], recv_sem=sr_sem.at[n],
            device_id={"tile": me // 8 * 8 + lax.rem(lax.rem(me, 8) + d, 8)}, device_id_type=MESH)

    def s2copy(n, d):
        return pltpu.make_async_remote_copy(
            src_ref=sc2_send.at[n], dst_ref=sc2_recv.at[n, d],
            send_sem=s2s_sem.at[n], recv_sem=s2r_sem.at[n],
            device_id=plane_peer(d), device_id_type=MESH)

    def collect(send, recv, ssem, rsem, n):
        rest = recv.at[n, pl.ds(1, recv.shape[1] - 1)]
        pltpu.make_async_remote_copy(
            src_ref=rest, dst_ref=rest, send_sem=ssem.at[n], recv_sem=rsem.at[n],
            device_id={"tile": lax.rem(me + 1, NTILE)}, device_id_type=MESH).wait()
        recv[n, 0] = send[n]
        return jnp.sum(recv[n], axis=0)

    def sum_start(n, gn, im):
        row = lax.broadcasted_iota(jnp.int32, (8, 128), 0)
        inn = sum(jnp.sum(i * i, axis=0, keepdims=True) for i in im)
        sc_send[n] = jnp.where(row == 0, gn, jnp.where(row == 1, inn, 0.0))
        for d in range(1, 8):
            scopy(n, d).start()

    def sum_middle(n):
        sc2_send[n] = collect(sc_send, sc_recv, ss_sem, sr_sem, n)
        for d in range(1, NPLANE):
            s2copy(n, d).start()

    def sum_end(n):
        both = jnp.sum(collect(sc2_send, sc2_recv, s2s_sem, s2r_sem, n), axis=1, keepdims=True)
        return both[0:1] / both[1:2]

    def setup_gram():
        @pl.loop(0, BLK)
        def _(r):
            t = lanes((1, NT))
            keep_ref[pl.ds(r, 1), :] = (t >= mute_ref[r]).astype(F32)

        gram = jnp.dot(keep_ref[...], prod_ref[...], precision=lax.Precision.HIGHEST, preferred_element_type=F32)
        lane = lanes((32, 128))
        left, real = lane < 64, even((32, 128))

        def col(a, b):
            i = a * 8 + b
            return jnp.where(left, gram[:32, i:i + 1], gram[32:, i:i + 1])

        for fo in range(NF):
            for fi in range(NF):
                gmap[fo, fi, 0] = jnp.where(real, col(fo, fi), col(4 + fo, 4 + fi))
                gmap[fo, fi, 1] = jnp.where(real, col(fo, 4 + fi), col(4 + fo, fi))

    def mix(e, h, spec):
        swapped = [swap(s) for s in spec]
        for fo in range(NF):
            o = jnp.zeros((32, 128), F32)
            for fi in range(NF):
                o += gmap[fo, fi, 0] * spec[fi] + gmap[fo, fi, 1] * swapped[fi]
            fsend[e, h, pl.ds(fo * 32, 32), :] = o

    def read_spec(ref):
        return [ref[pl.ds(f * 32, 32), :] for f in range(NF)]

    loads[0].wait()
    bb = bb_ref[...]
    quarter = even((4, 128))

    @pl.loop(0, BLK // 4)
    def _(k):
        low = pl.multiple_of(k * 128, 128)
        a, b = x_buf[pl.ds(low, 128), :], x_buf[pl.ds(BLK * 32 + low, 128), :]
        hi, lo = split(jnp.concatenate([a[:64], b[:64], a[64:], b[64:]], 0))
        o1 = dot(bb, hi, ((1,), (1,)))
        o2 = dot(bb, lo, ((1,), (1,)))
        o = o1[:8] + o1[8:] + o2[:8]
        for i in range(2):
            re, im = o[:4, i * 128:(i + 1) * 128], o[4:, i * 128:(i + 1) * 128]
            rows = pl.ds(k * 2 + i, 4, stride=32)
            fsend[0, 0, rows, :] = jnp.where(quarter, re, pltpu.roll(im, 32, 1))
            fsend[0, 1, rows, :] = jnp.where(quarter, pltpu.roll(re, 96, 1), im)

    pl.semaphore_wait(bar, NTILE - 1 + met)
    fstart(0, 0)
    fstart(0, 1)

    flat = jnp.concatenate([data_ref[c, h * 32:(h + 1) * 32, :] for h in range(2) for c in range(2)], 0).T
    for b in range(4):
        first, second = flat[b * 64:b * 64 + 32], flat[b * 64 + 32:b * 64 + 64]
        left = lanes((32, 128)) < 64
        r0_ref[0, b * 32:(b + 1) * 32, :] = jnp.where(left, first, pltpu.roll(second, 64, 1))
        r0_ref[1, b * 32:(b + 1) * 32, :] = jnp.where(left, pltpu.roll(first, 64, 1), second)

    loads[1].wait()

    @pl.loop(0, 2)
    def _(h):
        fwait(0, h)
        send_products(0, h, vt, frecv[0, h])

    loads[2].wait()
    setup_wide(ut, un)

    @pl.loop(0, 2)
    def _(h):
        r0_ref[h] = gather_products(0, h, un) - r0_ref[h]
        send_products(1, h, ut, r0_ref[h])

    setup_wide(vt, vn)
    setup_gram()

    def adjoint_and_back(e, use, between):
        k = NG // STEP - 1
        fsend[e, 0] = gather_products(e, 0, vn)
        fstart(e, 0)
        for i in range(k):
            gather_part(e, 1, vn, i)
        fwait(e, 0)
        use(0)
        fstart(e + 1, 0)
        gather_part(e, 1, vn, k)
        fsend[e, 1] = pack(acc[...])
        fstart(e, 1)
        between()
        fwait(e + 1, 0)
        right[...] = rhs(frecv[e + 1, 0], 1.0)
        for i in range(k):
            send_part(e + 1, 0, vt, i)
        fwait(e, 1)
        use(1)
        fstart(e + 1, 1)
        send_part(e + 1, 0, vt, k)
        fwait(e + 1, 1)
        send_products(e + 1, 1, vt, frecv[e + 1, 1])

    def first_use(h):
        spec0[h] = frecv[1, h]
        mix(2, h, read_spec(spec0.at[h]))
        gn_ref[h] = jnp.sum(spec0[h] * fsend[2, h], axis=0, keepdims=True)

    adjoint_and_back(1, first_use, lambda: None)

    im_ref[0] = gather_products(2, 0, un)
    send_products(3, 0, ut, im_ref[0])
    im_ref[1] = gather_products(2, 1, un)
    sum_start(0, gn_ref[0] + gn_ref[1], (im_ref[0], im_ref[1]))
    send_products(3, 1, ut, im_ref[1])

    adjoint_and_back(3, lambda h: mix(4, h, read_spec(frecv.at[3, h])), lambda: sum_middle(0))
    alpha0 = sum_end(0)
    for h in range(2):
        s1 = spec0[h] - alpha0 * frecv[3, h]
        gn_ref[h] = jnp.sum(s1 * (fsend[2, h] - alpha0 * fsend[4, h]), axis=0, keepdims=True)
        comb_ref[h] = s1
        r0_ref[h] = r0_ref[h] - alpha0 * im_ref[h]

    for h in range(2):
        im_ref[h] = im_ref[h] - alpha0 * gather_products(4, h, un)

    sum_start(1, gn_ref[0] + gn_ref[1], (im_ref[0], im_ref[1]))

    @pl.loop(0, 5)
    def _(e):
        for h in range(2):
            sent(e, h)

    sum_middle(1)
    alpha1 = sum_end(1)
    for h in range(2):
        comb_ref[h] = alpha0 * spec0[h] + alpha1 * comb_ref[h]
    blocks = []
    p0, p1 = (r0_ref[h] - alpha1 * im_ref[h] for h in range(2))
    for b in range(4):
        left = lanes((32, 128)) < 64
        a0, a1 = p0[b * 32:(b + 1) * 32], p1[b * 32:(b + 1) * 32]
        blocks.append(jnp.where(left, a0, pltpu.roll(a1, 64, 1)))
        blocks.append(jnp.where(left, pltpu.roll(a0, 64, 1), a1))
    flat = jnp.concatenate(blocks, 0).T
    for h in range(2):
        for c in range(2):
            resid_ref[c, h * 32:(h + 1) * 32, :] = flat[(h * 2 + c) * 32:(h * 2 + c + 1) * 32]


def update_kernel(mute_ref, comb_ref, b3_ref, x_ref, o_ref):
    g = pl.program_id(0)
    n = x_ref.shape[1]
    b3 = b3_ref[...]
    t = lanes((NV, NT))
    quarter = even((4, 128))
    for i in range(n):
        m = g * n + i
        p0, p1 = (comb_ref[h, pl.ds(m, 4, stride=32), :] for h in range(2))
        re = jnp.where(quarter, p0, pltpu.roll(p1, 32, 1))
        im = jnp.where(quarter, pltpu.roll(p0, 96, 1), p1)
        hi, lo = split(jnp.concatenate([re, im], 0))
        hi, lo = hi.astype(F32), lo.astype(F32)
        lhs = jnp.concatenate([hi, lo, hi, jnp.zeros_like(hi)], 0)
        grad = dot(lhs.T.astype(BF16), b3)
        for s in range(2):
            part = jnp.where(t >= mute_ref[s * 32 + m], grad[s * 64:(s + 1) * 64], 0.0)
            o_ref[s, i] = x_ref[s, i] - part


def body(x_time, mute, ranks, right_factor_columns, u_rows, data):
    b = basis()
    bhi, blo = split(jnp.asarray(b))
    bb = jnp.concatenate([bhi, blo], 0)
    b3 = jnp.concatenate([bhi, bhi, blo, jnp.zeros_like(bhi)], 0)
    prod = np.zeros((NT, 128), np.float32)
    prod[:, :64] = (b[:, None, :] * b[None, :, :]).reshape(64, NT).T
    vmem = pl.BlockSpec(memory_space=pltpu.VMEM)
    hbm = pl.BlockSpec(memory_space=pl.ANY)
    smem = pl.BlockSpec(memory_space=pltpu.SMEM)
    dma = pltpu.SemaphoreType.DMA
    tiles = jax.ShapeDtypeStruct((NG, 512, 512), BF16)
    vt, ut = pl.pallas_call(
        setup_kernel,
        out_shape=(tiles, tiles),
        in_specs=[smem, hbm, hbm],
        out_specs=(hbm, hbm),
        scratch_shapes=[
            pltpu.VMEM((2, 2, 256, NTILE * 64), F32),
            pltpu.VMEM((2, 2, 2, NTILE * 64, 128), F32),
            pltpu.VMEM((2, NG, 512, 512), BF16),
            pltpu.SMEM((2, NTILE), jnp.int32),
            dma((4,)), dma((2, NG)),
        ],
        compiler_params=pltpu.CompilerParams(vmem_limit_bytes=ROOM),
        name="setup",
    )(ranks[0], right_factor_columns[0, :, 0], u_rows[0, :, 0])
    pairs = (2, 128, 128)
    comb, resid = pl.pallas_call(
        main_kernel,
        out_shape=(jax.ShapeDtypeStruct(pairs, F32), jax.ShapeDtypeStruct((2, NV, NB), F32)),
        in_specs=[smem, hbm, hbm, hbm, vmem, vmem, vmem],
        out_specs=(vmem, vmem),
        scratch_shapes=[
            pltpu.VMEM((4096, 256), F32),
            pltpu.VMEM((NG, 512, 512), BF16),
            pltpu.VMEM((NG, 512, 512), BF16),
            pltpu.VMEM((NG, 512, 512), BF16),
            pltpu.VMEM((NG, 512, 512), BF16),
            pltpu.VMEM((5, 2, NTILE, 32, 128), F32),
            pltpu.VMEM((5, 2, NTILE, 32, 128), F32),
            pltpu.VMEM((5, *pairs), F32),
            pltpu.VMEM((5, *pairs), F32),
            pltpu.VMEM(pairs, F32),
            pltpu.VMEM((512, 128), BF16),
            pltpu.VMEM((512, 128), F32),
            pltpu.VMEM((BLK, NT), F32),
            pltpu.VMEM((NF, NF, 2, 32, 128), F32),
            pltpu.VMEM(pairs, F32),
            pltpu.VMEM(pairs, F32),
            pltpu.VMEM((2, 1, 128), F32),
            pltpu.VMEM((2, 8, 128), F32),
            pltpu.VMEM((2, 8, 8, 128), F32),
            pltpu.VMEM((2, 8, 128), F32),
            pltpu.VMEM((2, NPLANE, 8, 128), F32),
            dma((3,)), dma((5, 2)), dma((5, 2, NG // STEP)), dma((5, 2, NF)), dma((5, 2, NF)),
            dma((2,)), dma((2,)), dma((2,)), dma((2,)),
        ],
        compiler_params=pltpu.CompilerParams(collective_id=0, has_side_effects=True, vmem_limit_bytes=ROOM),
        name="descent",
    )(mute, x_time.reshape(4096, 256), vt, ut, data[0].swapaxes(1, 2), bb, jnp.asarray(prod))
    step = 16
    x_out = pl.pallas_call(
        update_kernel,
        grid=(32 // step,),
        out_shape=jax.ShapeDtypeStruct((2, 32, NV, NT), F32),
        in_specs=[
            smem, vmem, vmem,
            pl.BlockSpec((2, step, NV, NT), lambda i: (0, i, 0, 0)),
        ],
        out_specs=pl.BlockSpec((2, step, NV, NT), lambda i: (0, i, 0, 0)),
        compiler_params=pltpu.CompilerParams(vmem_limit_bytes=ROOM),
        name="update",
    )(mute, comb, b3, x_time.reshape(2, 32, NV, NT))
    return x_out.reshape(BLK, NV, NT), resid.swapaxes(1, 2)[None]


def solution(mesh):
    in_specs = (
        P(("tile", "freq"), None, None),
        P(("tile", "freq")),
        P("freq", None, None),
        P("freq", None, "tile", None, None),
        P("freq", None, "tile", None, None),
        P("freq", None, "tile", None),
    )
    out_specs = (P(("tile", "freq"), None, None), P("freq", None, "tile", None))
    return jax.shard_map(body, mesh=mesh, in_specs=in_specs, out_specs=out_specs, check_vma=False)
```
